32 devices in a mesh: wide: 8 (over z, core), narrow: 4 (over y, x).
Axes of the slice: x: 2, y: 2, z: 4, core: 2. Of those that a mesh axis runs over, the one named last changes fastest.
Arguments:
- features: bfloat16 [4, 1024, 128], P('narrow', 'wide'), may hold values from -6 to 6
- weight: bfloat16 [128, 128], replicated, may hold values from -0.5 to 0.5
- tiles: bfloat16 [4, 1024, 8, 128], P('narrow', 'wide'), may hold values from -0.25 to 0.25
- tile_cols: int32 [4, 8, 8], P('narrow'), may hold values from 0 to 7, as said below
- tile_counts: int32 [4, 8], P('narrow'), may hold values from 2 to 8, as said below
- cotangent: bfloat16 [4, 1024, 128], P('narrow', 'wide'), may hold values from -6 to 6
Outputs:
- activated: bfloat16 [4, 1024, 128], P('narrow', 'wide')
- feature_grad: bfloat16 [4, 1024, 128], P('narrow', 'wide')
- weight_grad: float32 [128, 128], P('wide')
The draws below stay inside these ranges and needn't reach their ends.
Inputs may be any that keep to these rules, and one draw needn't show every extreme that they name: `tile_cols`: slot 0 of each block row holds that block row's own diagonal tile (its column equals the block row); other slots may name any block column of the group, also repeatedly. `tile_counts`: each group has a block row that uses all 8 slots.
All inputs are finite; a program needn't handle non-finite values.
Results may differ from the reference program's by a relative error of at most 0.0062.
Values may be sent and summed in bfloat16 or wider, within the bound.
A program may use at most 64 MiB of HBM per device.

```python
import jax
import jax.numpy as jnp
from jax import lax

D = 128
TILE = 128
SLOTS = 8
GROUPS = 4
GROUP_NODES = 1024
BLOCKS = 8


def draw_tile_cols(key, part):
    key = jax.random.fold_in(key, 11)
    chosen_cols = jax.random.randint(key, (GROUPS, BLOCKS, SLOTS), 0, BLOCKS)
    own_block = jnp.broadcast_to(jnp.arange(BLOCKS, dtype=jnp.int32)[None, :, None], (GROUPS, BLOCKS, SLOTS))
    first_slot = jnp.arange(SLOTS)[None, None, :] == 0
    return jnp.where(first_slot, own_block, chosen_cols).astype(jnp.int32)


def draw_tile_counts(key, part):
    key = jax.random.fold_in(key, 12)
    key_count, key_full = jax.random.split(key)
    drawn_counts = jax.random.randint(key_count, (GROUPS, BLOCKS), 2, SLOTS + 1)
    fullest = jax.random.randint(key_full, (GROUPS,), 0, BLOCKS)
    full_row = jnp.arange(BLOCKS)[None, :] == fullest[:, None]
    return jnp.where(full_row, SLOTS, drawn_counts).astype(jnp.int32)


def raised(array, own_key, source, target, parts, factor):
    def block_of(dim):
        return (jnp.arange(array.shape[dim]) // (array.shape[dim] // parts)).reshape((-1,) + (1,) * (array.ndim - 1 - dim))

    near = jax.random.permutation(own_key, parts)[block_of(target)]
    second = (block_of(target) + parts // 2) % parts
    return jnp.where((block_of(source) == near) | (block_of(source) == second), factor * array, array)


def block_levels(own_key, extent, cuts, smallest, largest):
    gain, own = 1.0, jax.random.fold_in(own_key, 6)
    for position, blocks in cuts:
        heights = jnp.exp(jax.random.uniform(jax.random.fold_in(own, position), (blocks,), jnp.float32, smallest / len(cuts), largest / len(cuts)))
        gain = gain * jnp.repeat(heights, extent[position] // blocks).reshape([-1 if axis == position else 1 for axis in range(len(extent))])
    return gain


def noise(key, dims, scale, most, pieces=(), kind=jnp.bfloat16):
    result = scale * jax.random.normal(key, dims, jnp.float32)
    if pieces:
        result = result * block_levels(key, dims, pieces, -0.22, 0.18)
    return jnp.clip(result, -most, most).astype(kind)


def heavy_noise(key, extent, deviation, most, cuts, heavy, kind=jnp.bfloat16):
    values = deviation * jax.random.normal(key, extent, jnp.float32)
    if cuts:
        values = values * block_levels(key, extent, cuts, -0.22, 0.18)
    return jnp.clip(raised(values, jax.random.fold_in(key, 3), *heavy), -most, most).astype(kind)


def setup_inputs(seed: int = 0) -> dict:
    splits = jax.random.split(jax.random.key(seed), 7)
    features = heavy_noise(splits[0], (GROUPS, GROUP_NODES, D), 1.0, 6.0, ((0, 4), (1, 8)), (1, 2, 8, 2.0))
    weight = noise(splits[1], (D, D), D ** -0.5, 0.5)
    tiles = noise(splits[2], (GROUPS, GROUP_NODES, SLOTS, TILE), (TILE * SLOTS // 2) ** -0.5, 0.25, ((0, 4), (1, 8)))
    tile_cols = draw_tile_cols(jax.random.fold_in(splits[6], 71), 0)
    tile_counts = draw_tile_counts(jax.random.fold_in(splits[6], 71), 0)
    cotangent = noise(splits[5], (GROUPS, GROUP_NODES, D), 1.0, 6.0, ((0, 4), (1, 8)))
    return {"features": features, "weight": weight, "tiles": tiles, "tile_cols": tile_cols, "tile_counts": tile_counts, "cotangent": cotangent}


def group_pass(feat_block, weight, tile_block, col_block, count_block, cot_block):
    block_count = col_block.shape[0]
    slot_count = col_block.shape[1]
    tile_size = tile_block.shape[2]
    node_count = feat_block.shape[0]
    feat_width = feat_block.shape[1]
    projected = jnp.dot(feat_block, weight, preferred_element_type=jnp.float32).astype(jnp.bfloat16)
    alive_mask = jnp.arange(slot_count)[None, :] < count_block[:, None]
    stacked = projected.reshape(block_count, tile_size, feat_width)
    picked = stacked[col_block] * alive_mask[:, :, None, None].astype(jnp.bfloat16)
    tile_rows = tile_block.reshape(block_count, tile_size, slot_count, tile_size).astype(jnp.float32)
    pre_act = jnp.einsum('bnst,bstd->bnd', tile_rows, picked.astype(jnp.float32))
    pre_act = pre_act.reshape(node_count, feat_width)
    sig_val = jax.nn.sigmoid(pre_act)
    activated = (pre_act * sig_val).astype(jnp.bfloat16)
    act_grad = (cot_block.astype(jnp.float32) * sig_val * (1.0 + pre_act * (1.0 - sig_val))).astype(jnp.bfloat16)
    contrib = jnp.einsum('bnst,bnd->bstd', tile_rows,
                         act_grad.reshape(block_count, tile_size, feat_width).astype(jnp.float32))
    seg_ids = jnp.where(alive_mask, col_block, block_count).reshape(-1).astype(jnp.int32)
    summed = jax.ops.segment_sum(contrib.reshape(block_count * slot_count, tile_size, feat_width),
                                 seg_ids, num_segments=block_count + 1)
    proj_grad = summed[:block_count].reshape(node_count, feat_width).astype(jnp.bfloat16)
    feature_grad = jnp.dot(proj_grad, weight.T, preferred_element_type=jnp.float32).astype(jnp.bfloat16)
    weight_part = jnp.dot(feat_block.T, proj_grad, preferred_element_type=jnp.float32)
    return activated, feature_grad, weight_part


def reference(features, weight, tiles, tile_cols, tile_counts, cotangent):
    def one_group(items):
        return group_pass(items[0], weight, items[1], items[2], items[3], items[4])

    activated, feature_grad, weight_parts = lax.map(one_group, (features, tiles, tile_cols, tile_counts, cotangent))
    return activated, feature_grad, jnp.sum(weight_parts, axis=0)
```

```python
import functools

import jax
import jax.numpy as jnp
from jax import lax
from jax.experimental import pallas as pl
from jax.experimental.pallas import tpu as pltpu
from jax.sharding import PartitionSpec as P

MESH = pl.DeviceIdType.MESH
F32 = jnp.float32
BF16 = jnp.bfloat16


def selection(cols_ref, counts_ref, me, blocks, slots, chunk):
    shape = (blocks * chunk, chunk * slots)
    row = lax.broadcasted_iota(jnp.int32, shape, 0)
    lane = lax.broadcasted_iota(jnp.int32, (1, chunk * slots), 1)
    slot = lax.rem(lane, slots)
    node = lane // slots
    counts = counts_ref[...]
    here = lax.broadcasted_iota(jnp.int32, counts.shape, 1) == me
    count = jnp.sum(jnp.where(here, counts, 0), axis=1, keepdims=True)
    cols = cols_ref[0, pl.ds(me, 1), :]
    wanted = jnp.zeros((1, chunk * slots), jnp.int32)
    for s in range(slots):
        wanted = jnp.where(slot == s, cols[:, s:s + 1], wanted)
    wanted = jnp.where(slot < count, wanted * chunk + node, -1)
    return jnp.where(row == wanted, 1.0, 0.0).astype(BF16)


def kernel(
    wide, narrow, slots,
    cols_hbm, counts_hbm, feat_hbm, weight_hbm, tiles_hbm, cot_hbm,
    act_ref, fgrad_ref, wgrad_ref,
    cols_ref, counts_ref, weight_ref, tiles_ref, cot_ref, in_sems, gathered, adj, terms, incoming, wpart, wincoming, nbuf,
    f_send, f_recv, t_send, t_recv, w_send, w_recv, n_send, n_recv,
):
    me = lax.axis_index("wide")
    grp = lax.axis_index("narrow")
    nodes = feat_hbm.shape[1]
    tile = tiles_hbm.shape[1]
    chunk = tile // slots
    share = wgrad_ref.shape[0]

    def wide_peer(k):
        return lax.rem(me + k, wide)

    def narrow_peer(j):
        return lax.rem(grp + j, narrow)

    barrier = pltpu.get_barrier_semaphore()
    for k in range(1, wide):
        pl.semaphore_signal(barrier, inc=1, device_id={"wide": wide_peer(k)}, device_id_type=MESH)
    for j in range(1, narrow):
        pl.semaphore_signal(barrier, inc=1, device_id={"narrow": narrow_peer(j)}, device_id_type=MESH)

    def rows_of(index):
        return pl.ds(pl.multiple_of(index * tile, tile), tile)

    loads = [
        pltpu.make_async_copy(src, dst, in_sems.at[i])
        for i, (src, dst) in enumerate((
            (cols_hbm, cols_ref), (counts_hbm, counts_ref), (tiles_hbm, tiles_ref),
            (feat_hbm.at[0], gathered.at[rows_of(me)]), (weight_hbm, weight_ref), (cot_hbm, cot_ref)))
    ]
    for load in loads:
        load.start()
    pl.semaphore_wait(barrier, wide - 1 + narrow - 1)

    def feat_copy(slot, k):
        return pltpu.make_async_remote_copy(
            src_ref=feat_hbm.at[0], dst_ref=gathered.at[rows_of(slot)],
            send_sem=f_send.at[k - 1], recv_sem=f_recv.at[k - 1],
            device_id={"wide": wide_peer(k)}, device_id_type=MESH)

    for k in range(1, wide):
        feat_copy(me, k).start()
    for load in loads:
        load.wait()

    pick = selection(cols_ref, counts_ref, me, wide, slots, chunk)
    for j in range(nodes // chunk):
        part = jnp.dot(pick, tiles_ref[j * tile:(j + 1) * tile, :], preferred_element_type=F32).astype(BF16)
        for c in range(wide):
            adj[j * chunk:(j + 1) * chunk, c * tile:(c + 1) * tile] = part[c * chunk:(c + 1) * chunk]

    for k in range(1, wide):
        feat_copy(lax.rem(me - k + wide, wide), k).wait_recv()

    mixed = jnp.dot(adj[...], gathered[...], preferred_element_type=F32)
    mixed_hi = mixed.astype(BF16)
    mixed_lo = (mixed - mixed_hi.astype(F32)).astype(BF16)
    weight = weight_ref[...]
    pre_act = (jnp.dot(mixed_hi, weight, preferred_element_type=F32)
               + jnp.dot(mixed_lo, weight, preferred_element_type=F32))
    sig_val = jax.nn.sigmoid(pre_act)
    act_ref[0] = (pre_act * sig_val).astype(BF16)
    act_grad = (cot_ref[0].astype(F32) * sig_val * (1.0 + pre_act * (1.0 - sig_val))).astype(BF16)

    back = lax.dot_general(weight, act_grad, (((1,), (1,)), ((), ())), preferred_element_type=F32).astype(BF16)

    def term_copy(dest, k):
        return pltpu.make_async_remote_copy(
            src_ref=terms.at[dest], dst_ref=incoming.at[k - 1],
            send_sem=t_send.at[k - 1], recv_sem=t_recv.at[k - 1],
            device_id={"wide": wide_peer(k)}, device_id_type=MESH)

    for k in range(1, wide):
        dest = wide_peer(k)
        terms[dest] = jnp.dot(back, adj[:, rows_of(dest)], preferred_element_type=F32).astype(BF16)
        term_copy(dest, k).start()

    def weight_copy(dest, k):
        return pltpu.make_async_remote_copy(
            src_ref=wpart.at[dest], dst_ref=wincoming.at[k - 1],
            send_sem=w_send.at[k - 1], recv_sem=w_recv.at[k - 1],
            device_id={"wide": wide_peer(k)}, device_id_type=MESH)

    weight_part = lax.dot_general(
        mixed_hi, act_grad, (((0,), (0,)), ((), ())), preferred_element_type=F32)
    for c in range(wide):
        wpart[c] = weight_part[c * share:(c + 1) * share]
    for k in range(1, wide):
        weight_copy(wide_peer(k), k).start()

    own = jnp.dot(back, adj[:, rows_of(me)], preferred_element_type=F32)

    wsum = wpart[me]
    for k in range(1, wide):
        weight_copy(wide_peer(k), k).wait_recv()
        wsum = wsum + wincoming[k - 1]
    nbuf[grp] = wsum

    def narrow_copy(slot, j):
        return pltpu.make_async_remote_copy(
            src_ref=nbuf.at[slot], dst_ref=nbuf.at[slot],
            send_sem=n_send.at[j - 1], recv_sem=n_recv.at[j - 1],
            device_id={"narrow": narrow_peer(j)}, device_id_type=MESH)

    for j in range(1, narrow):
        narrow_copy(grp, j).start()

    for k in range(1, wide):
        term_copy(wide_peer(k), k).wait_recv()
        own = own + incoming[k - 1].astype(F32)
    fgrad_ref[0] = own.T.astype(BF16)

    for j in range(1, narrow):
        narrow_copy(lax.rem(grp - j + narrow, narrow), j).wait_recv()
    total = nbuf[0]
    for j in range(1, narrow):
        total = total + nbuf[j]
    wgrad_ref[...] = total

    for k in range(1, wide):
        feat_copy(me, k).wait_send()
        term_copy(wide_peer(k), k).wait_send()
        weight_copy(wide_peer(k), k).wait_send()
    for j in range(1, narrow):
        narrow_copy(grp, j).wait_send()


def shards(wide, narrow, features, weight, tiles, tile_cols, tile_counts, cotangent):
    _, nodes, width = features.shape
    slots, tile = tiles.shape[2:]
    if nodes != tile:
        raise ValueError("block rows")
    share = width // wide
    vmem = pl.BlockSpec(memory_space=pltpu.VMEM)
    hbm = pl.BlockSpec(memory_space=pltpu.HBM)
    dma = pltpu.SemaphoreType.DMA
    flops = 2 * nodes * tile * width * (2 * wide + wide + 4)
    return pl.pallas_call(
        functools.partial(kernel, wide, narrow, slots),
        out_shape=(
            jax.ShapeDtypeStruct((1, nodes, width), BF16),
            jax.ShapeDtypeStruct((1, nodes, width), BF16),
            jax.ShapeDtypeStruct((share, width), F32),
        ),
        in_specs=[hbm] * 6,
        out_specs=(vmem, vmem, vmem),
        scratch_shapes=[
            pltpu.VMEM(tile_cols.shape, jnp.int32),
            pltpu.VMEM(tile_counts.shape, jnp.int32),
            pltpu.VMEM(weight.shape, BF16),
            pltpu.VMEM((nodes * slots, tile), BF16),
            pltpu.VMEM(cotangent.shape, BF16),
            dma((6,)),
            pltpu.VMEM((wide * tile, width), BF16),
            pltpu.VMEM((nodes, wide * tile), BF16),
            pltpu.VMEM((wide, width, tile), BF16),
            pltpu.VMEM((wide - 1, width, tile), BF16),
            pltpu.VMEM((wide, share, width), F32),
            pltpu.VMEM((wide - 1, share, width), F32),
            pltpu.VMEM((narrow, share, width), F32),
            dma((wide - 1,)), dma((wide - 1,)),
            dma((wide - 1,)), dma((wide - 1,)),
            dma((wide - 1,)), dma((wide - 1,)),
            dma((narrow - 1,)), dma((narrow - 1,)),
        ],
        compiler_params=pltpu.CompilerParams(
            collective_id=0, has_side_effects=True, vmem_limit_bytes=32 * 1024 * 1024),
        cost_estimate=pl.CostEstimate(
            flops=flops, bytes_accessed=2 * nodes * width * (slots + 4), transcendentals=nodes * width),
        name="graph_layer",
    )(tile_cols, tile_counts, features, weight, tiles.reshape(nodes * slots, tile), cotangent)


def solution(mesh):
    placed = (
        P("narrow", "wide", None),
        P(),
        P("narrow", "wide", None, None),
        P("narrow", None, None),
        P("narrow", None),
        P("narrow", "wide", None),
    )
    return jax.shard_map(
        functools.partial(shards, mesh.shape["wide"], mesh.shape["narrow"]),
        mesh=mesh,
        in_specs=placed,
        out_specs=(P("narrow", "wide", None), P("narrow", "wide", None), P("wide", None)),
        check_vma=False,
    )
```

```python
import functools

import jax
import jax.numpy as jnp
from jax import lax
from jax.experimental import pallas as pl
from jax.experimental.pallas import tpu as pltpu
from jax.sharding import PartitionSpec as P

MESH = pl.DeviceIdType.MESH
F32 = jnp.float32
BF16 = jnp.bfloat16
VMEM_LIMIT = 60 * 1024 * 1024


def selection(cols_ref, counts_ref, row_block, blocks, slots, chunk):
    shape = (blocks * chunk, chunk * slots)
    row = lax.broadcasted_iota(jnp.int32, shape, 0)
    lane = lax.broadcasted_iota(jnp.int32, (1, chunk * slots), 1)
    slot = lax.rem(lane, slots)
    node = lane // slots
    counts = counts_ref[...]
    here = lax.broadcasted_iota(jnp.int32, counts.shape, 1) == row_block
    count = jnp.sum(jnp.where(here, counts, 0), axis=1, keepdims=True)
    cols = cols_ref[0, pl.ds(row_block, 1), :]
    wanted = jnp.zeros((1, chunk * slots), jnp.int32)
    for s in range(slots):
        wanted = jnp.where(slot == s, cols[:, s:s + 1], wanted)
    wanted = jnp.where(slot < count, wanted * chunk + node, -1)
    return jnp.where(row == wanted, 1.0, 0.0).astype(BF16)


def partner(z, k):
    bit, out = 1, z
    while bit <= k:
        if k & bit:
            out = out + bit - 2 * bit * lax.rem(z // bit, 2)
        bit *= 2
    return out


def partner_order(count):
    order, half = [], count // 2
    while half:
        order += list(range(half, 2 * half))
        half //= 2
    return order


def kernel(
    wide, narrow, slots,
    cols_hbm, counts_hbm, feat_hbm, weight_hbm, tiles_hbm, cot_hbm,
    act_ref, fgrad_ref, wgrad_ref,
    cols_ref, counts_ref, weight_ref, tiles_ref, cot_ref, gathered, adj, acts, terms, incoming, wpart, wincoming, nbuf,
    in_sems, f_send, f_recv, x_send, x_recv, s_send, s_recv, t_send, t_recv, w_send, w_recv, n_send, n_recv,
):
    me = lax.axis_index("wide")
    grp = lax.axis_index("narrow")
    zs = wide // 2
    z, core = me // 2, lax.rem(me, 2)
    other = 1 - core
    sibling = 2 * z + other
    nodes = feat_hbm.shape[1]
    tile = tiles_hbm.shape[1]
    chunk = tile // slots
    share = wgrad_ref.shape[0]
    order = partner_order(zs)

    def peer(k):
        return 2 * partner(z, k) + core

    def narrow_peer(j):
        return lax.rem(grp + j, narrow)

    barrier = pltpu.get_barrier_semaphore()
    for k in order:
        pl.semaphore_signal(barrier, inc=1, device_id={"wide": peer(k)}, device_id_type=MESH)
    pl.semaphore_signal(barrier, inc=1, device_id={"wide": sibling}, device_id_type=MESH)
    for j in range(1, narrow):
        pl.semaphore_signal(barrier, inc=1, device_id={"narrow": narrow_peer(j)}, device_id_type=MESH)

    def rows_of(index):
        return pl.ds(pl.multiple_of(index * tile, tile), tile)

    loads = [
        pltpu.make_async_copy(src, dst, in_sems.at[i])
        for i, (src, dst) in enumerate((
            (cols_hbm, cols_ref), (counts_hbm, counts_ref), (tiles_hbm, tiles_ref.at[core]),
            (feat_hbm.at[0], gathered.at[rows_of(me)]), (weight_hbm, weight_ref),
            (cot_hbm.at[0], cot_ref.at[core])))
    ]
    for load in loads:
        load.start()
    pl.semaphore_wait(barrier, zs + narrow - 1)

    def feat_copy(k, slot):
        return pltpu.make_async_remote_copy(
            src_ref=feat_hbm.at[0], dst_ref=gathered.at[rows_of(slot)],
            send_sem=f_send.at[k - 1], recv_sem=f_recv.at[k - 1],
            device_id={"wide": peer(k)}, device_id_type=MESH)

    def forward_copy(k, slot):
        return pltpu.make_async_remote_copy(
            src_ref=gathered.at[rows_of(slot)], dst_ref=gathered.at[rows_of(slot)],
            send_sem=x_send.at[k - 1], recv_sem=x_recv.at[k - 1],
            device_id={"wide": sibling}, device_id_type=MESH)

    def swap_copies(half, slot):
        pairs = ((tiles_hbm, tiles_ref.at[half]), (feat_hbm.at[0], gathered.at[rows_of(slot)]),
                 (cot_hbm.at[0], cot_ref.at[half]))
        return [
            pltpu.make_async_remote_copy(
                src_ref=src, dst_ref=dst, send_sem=s_send.at[i], recv_sem=s_recv.at[i],
                device_id={"wide": sibling}, device_id_type=MESH)
            for i, (src, dst) in enumerate(pairs)
        ]

    for k in order:
        feat_copy(k, me).start()
    for copy in swap_copies(core, me):
        copy.start()
    for load in loads:
        load.wait()

    def build(half):
        pick = selection(cols_ref, counts_ref, 2 * z + half, wide, slots, chunk)
        base = half * nodes
        for j in range(nodes // chunk):
            part = jnp.dot(
                pick, tiles_ref[half, j * tile:(j + 1) * tile, :], preferred_element_type=F32).astype(BF16)
            rows = pl.ds(pl.multiple_of(base + j * chunk, chunk), chunk)
            for c in range(wide):
                adj[rows, c * tile:(c + 1) * tile] = part[c * chunk:(c + 1) * chunk]

    build(core)
    swapped = swap_copies(other, sibling)
    swapped[0].wait_recv()
    build(other)
    for k in order:
        feat_copy(k, peer(k)).wait_recv()
        forward_copy(k, peer(k)).start()
    swapped[1].wait_recv()
    swapped[2].wait_recv()
    for k in order:
        forward_copy(k, 2 * partner(z, k) + other).wait_recv()

    mixed = jnp.dot(adj[...], gathered[...], preferred_element_type=F32)
    mixed_hi = mixed.astype(BF16)
    mixed_lo = (mixed - mixed_hi.astype(F32)).astype(BF16)
    weight = weight_ref[...]
    pre_act = (jnp.dot(mixed_hi, weight, preferred_element_type=F32)
               + jnp.dot(mixed_lo, weight, preferred_element_type=F32))
    sig_val = jax.nn.sigmoid(pre_act)
    acts[...] = (pre_act * sig_val).astype(BF16).reshape(acts.shape)
    cot = cot_ref[...].reshape(2 * nodes, -1).astype(F32)
    act_grad = (cot * sig_val * (1.0 + pre_act * (1.0 - sig_val))).astype(BF16)

    def weight_copy(k):
        return pltpu.make_async_remote_copy(
            src_ref=wpart.at[peer(k)], dst_ref=wincoming.at[k - 1],
            send_sem=w_send.at[k - 1], recv_sem=w_recv.at[k - 1],
            device_id={"wide": peer(k)}, device_id_type=MESH)

    weight_part = lax.dot_general(
        mixed_hi, act_grad, (((0,), (0,)), ((), ())), preferred_element_type=F32)
    for c in range(wide):
        wpart[c] = weight_part[c * share:(c + 1) * share]
    for k in order:
        weight_copy(k).start()

    back = lax.dot_general(weight, act_grad, (((1,), (1,)), ((), ())), preferred_element_type=F32).astype(BF16)

    def term_copy(k):
        return pltpu.make_async_remote_copy(
            src_ref=terms.at[k - 1], dst_ref=incoming.at[k - 1],
            send_sem=t_send.at[k - 1], recv_sem=t_recv.at[k - 1],
            device_id={"wide": peer(k)}, device_id_type=MESH)

    for k in order:
        terms[k - 1] = jnp.dot(back, adj[:, rows_of(peer(k))], preferred_element_type=F32).astype(BF16)
        term_copy(k).start()

    own = jnp.dot(back, adj[:, rows_of(me)], preferred_element_type=F32)
    act_ref[0] = acts[core]

    wsum = wpart[me]
    for k in order:
        weight_copy(k).wait_recv()
        wsum = wsum + wincoming[k - 1]
    nbuf[grp] = wsum

    def narrow_copy(j, slot):
        return pltpu.make_async_remote_copy(
            src_ref=nbuf.at[slot], dst_ref=nbuf.at[slot],
            send_sem=n_send.at[j - 1], recv_sem=n_recv.at[j - 1],
            device_id={"narrow": narrow_peer(j)}, device_id_type=MESH)

    for j in range(1, narrow):
        narrow_copy(j, grp).start()

    for k in order:
        term_copy(k).wait_recv()
        own = own + incoming[k - 1].astype(F32)
    fgrad_ref[0] = own.T.astype(BF16)

    for j in range(1, narrow):
        narrow_copy(j, lax.rem(grp - j + narrow, narrow)).wait_recv()
    total = nbuf[0]
    for j in range(1, narrow):
        total = total + nbuf[j]
    wgrad_ref[...] = total

    for copy in swap_copies(core, me):
        copy.wait_send()
    for k in order:
        feat_copy(k, me).wait_send()
        forward_copy(k, peer(k)).wait_send()
        weight_copy(k).wait_send()
        term_copy(k).wait_send()
    for j in range(1, narrow):
        narrow_copy(j, grp).wait_send()


def shards(wide, narrow, features, weight, tiles, tile_cols, tile_counts, cotangent):
    _, nodes, width = features.shape
    slots, tile = tiles.shape[2:]
    zs = wide // 2
    if nodes != tile or 2 * zs != wide or zs & (zs - 1):
        raise ValueError("mesh shape")
    share = width // wide
    vmem = pl.BlockSpec(memory_space=pltpu.VMEM)
    hbm = pl.BlockSpec(memory_space=pltpu.HBM)
    dma = pltpu.SemaphoreType.DMA
    flops = 2 * nodes * tile * width * (5 * wide + 8)
    return pl.pallas_call(
        functools.partial(kernel, wide, narrow, slots),
        out_shape=(
            jax.ShapeDtypeStruct((1, nodes, width), BF16),
            jax.ShapeDtypeStruct((1, nodes, width), BF16),
            jax.ShapeDtypeStruct((share, width), F32),
        ),
        in_specs=[hbm] * 6,
        out_specs=(vmem, vmem, vmem),
        scratch_shapes=[
            pltpu.VMEM(tile_cols.shape, jnp.int32),
            pltpu.VMEM(tile_counts.shape, jnp.int32),
            pltpu.VMEM(weight.shape, BF16),
            pltpu.VMEM((2, nodes * slots, tile), BF16),
            pltpu.VMEM((2, nodes, width), BF16),
            pltpu.VMEM((wide * tile, width), BF16),
            pltpu.VMEM((2 * nodes, wide * tile), BF16),
            pltpu.VMEM((2, nodes, width), BF16),
            pltpu.VMEM((zs - 1, width, tile), BF16),
            pltpu.VMEM((zs - 1, width, tile), BF16),
            pltpu.VMEM((wide, share, width), F32),
            pltpu.VMEM((zs - 1, share, width), F32),
            pltpu.VMEM((narrow, share, width), F32),
            dma((6,)),
            dma((zs - 1,)), dma((zs - 1,)),
            dma((zs - 1,)), dma((zs - 1,)),
            dma((3,)), dma((3,)),
            dma((zs - 1,)), dma((zs - 1,)),
            dma((zs - 1,)), dma((zs - 1,)),
            dma((narrow - 1,)), dma((narrow - 1,)),
        ],
        compiler_params=pltpu.CompilerParams(
            collective_id=0, has_side_effects=True, vmem_limit_bytes=VMEM_LIMIT),
        cost_estimate=pl.CostEstimate(
            flops=flops, bytes_accessed=2 * nodes * width * (slots + 4), transcendentals=2 * nodes * width),
        name="graph_layer",
    )(tile_cols, tile_counts, features, weight, tiles.reshape(nodes * slots, tile), cotangent)


def solution(mesh):
    placed = (
        P("narrow", "wide", None),
        P(),
        P("narrow", "wide", None, None),
        P("narrow", None, None),
        P("narrow", None),
        P("narrow", "wide", None),
    )
    return jax.shard_map(
        functools.partial(shards, mesh.shape["wide"], mesh.shape["narrow"]),
        mesh=mesh,
        in_specs=placed,
        out_specs=(P("narrow", "wide", None), P("narrow", "wide", None), P("wide", None)),
        check_vma=False,
    )
```

```python
import functools

import jax
import jax.numpy as jnp
from jax import lax
from jax.experimental import pallas as pl
from jax.experimental.pallas import tpu as pltpu
from jax.sharding import PartitionSpec as P

MESH = pl.DeviceIdType.MESH
F32 = jnp.float32
BF16 = jnp.bfloat16
VMEM_LIMIT = 32 * 1024 * 1024


def selection(cols_ref, counts_ref, row_block, blocks, slots, chunk):
    shape = (blocks * chunk, chunk * slots)
    row = lax.broadcasted_iota(jnp.int32, shape, 0)
    lane = lax.broadcasted_iota(jnp.int32, (1, chunk * slots), 1)
    slot = lax.rem(lane, slots)
    node = lane // slots
    counts = counts_ref[...]
    here = lax.broadcasted_iota(jnp.int32, counts.shape, 1) == row_block
    count = jnp.sum(jnp.where(here, counts, 0), axis=1, keepdims=True)
    cols = cols_ref[0, pl.ds(row_block, 1), :]
    wanted = jnp.zeros((1, chunk * slots), jnp.int32)
    for s in range(slots):
        wanted = jnp.where(slot == s, cols[:, s:s + 1], wanted)
    wanted = jnp.where(slot < count, wanted * chunk + node, -1)
    return jnp.where(row == wanted, 1.0, 0.0).astype(BF16)


def partner(z, k):
    bit, out = 1, z
    while bit <= k:
        if k & bit:
            out = out + bit - 2 * bit * lax.rem(z // bit, 2)
        bit *= 2
    return out


def partner_order(count):
    order, half = [], count // 2
    while half:
        order += list(range(half, 2 * half))
        half //= 2
    return order


def kernel(
    wide, narrow, slots,
    cols_hbm, counts_hbm, feat_hbm, weight_hbm, tiles_hbm, cot_hbm,
    act_ref, fgrad_ref, wgrad_ref,
    cols_ref, counts_ref, weight_ref, tiles_ref, cot_ref, gathered, adj, acts, terms, incoming, wpart, wincoming, nbuf,
    in_sems, f_send, f_recv, x_send, x_recv, s_send, s_recv, t_send, t_recv, w_send, w_recv, n_send, n_recv,
):
    me = lax.axis_index("wide")
    grp = lax.axis_index("narrow")
    zs = wide // 2
    z, core = me // 2, lax.rem(me, 2)
    other = 1 - core
    sibling = 2 * z + other
    across = 2 * partner(z, 1) + other
    nodes = feat_hbm.shape[1]
    tile = tiles_hbm.shape[1]
    chunk = tile // slots
    share = wgrad_ref.shape[0]
    order = partner_order(zs)

    def peer(k):
        return 2 * partner(z, k) + core

    def narrow_peer(j):
        return lax.rem(grp + j, narrow)

    barrier = pltpu.get_barrier_semaphore()
    for k in order:
        pl.semaphore_signal(barrier, inc=1, device_id={"wide": peer(k)}, device_id_type=MESH)
    for device in (sibling, across):
        pl.semaphore_signal(barrier, inc=1, device_id={"wide": device}, device_id_type=MESH)
    for j in range(1, narrow):
        pl.semaphore_signal(barrier, inc=1, device_id={"narrow": narrow_peer(j)}, device_id_type=MESH)

    def rows_of(index):
        return pl.ds(pl.multiple_of(index * tile, tile), tile)

    loads = [
        pltpu.make_async_copy(src, dst, in_sems.at[i])
        for i, (src, dst) in enumerate((
            (cols_hbm, cols_ref), (counts_hbm, counts_ref), (tiles_hbm, tiles_ref.at[core]),
            (feat_hbm.at[0], gathered.at[rows_of(me)]), (weight_hbm, weight_ref),
            (cot_hbm.at[0], cot_ref.at[core])))
    ]
    for load in loads:
        load.start()
    pl.semaphore_wait(barrier, zs + narrow)

    def feat_copy(k, slot):
        return pltpu.make_async_remote_copy(
            src_ref=feat_hbm.at[0], dst_ref=gathered.at[rows_of(slot)],
            send_sem=f_send.at[k - 1], recv_sem=f_recv.at[k - 1],
            device_id={"wide": peer(k)}, device_id_type=MESH)

    def across_copy(slot):
        return pltpu.make_async_remote_copy(
            src_ref=feat_hbm.at[0], dst_ref=gathered.at[rows_of(slot)],
            send_sem=f_send.at[zs - 1], recv_sem=f_recv.at[zs - 1],
            device_id={"wide": across}, device_id_type=MESH)

    def forward_copy(k, slot):
        return pltpu.make_async_remote_copy(
            src_ref=gathered.at[rows_of(slot)], dst_ref=gathered.at[rows_of(slot)],
            send_sem=x_send.at[k - 1], recv_sem=x_recv.at[k - 1],
            device_id={"wide": sibling}, device_id_type=MESH)

    def swap_copies(half, slot):
        pairs = ((tiles_hbm, tiles_ref.at[half]), (feat_hbm.at[0], gathered.at[rows_of(slot)]),
                 (cot_hbm.at[0], cot_ref.at[half]))
        return [
            pltpu.make_async_remote_copy(
                src_ref=src, dst_ref=dst, send_sem=s_send.at[i], recv_sem=s_recv.at[i],
                device_id={"wide": sibling}, device_id_type=MESH)
            for i, (src, dst) in enumerate(pairs)
        ]

    for k in order:
        feat_copy(k, me).start()
    across_copy(me).start()
    for copy in swap_copies(core, me):
        copy.start()
    for load in loads:
        load.wait()

    def build(half):
        pick = selection(cols_ref, counts_ref, 2 * z + half, wide, slots, chunk)
        base = half * nodes
        for j in range(nodes // chunk):
            part = jnp.dot(
                pick, tiles_ref[half, j * tile:(j + 1) * tile, :], preferred_element_type=F32).astype(BF16)
            rows = pl.ds(pl.multiple_of(base + j * chunk, chunk), chunk)
            for c in range(wide):
                adj[rows, c * tile:(c + 1) * tile] = part[c * chunk:(c + 1) * chunk]

    def mix(chip):
        span = pl.ds(pl.multiple_of(chip * 2 * tile, 2 * tile), 2 * tile)
        return jnp.dot(adj[:, span], gathered[span, :], preferred_element_type=F32)

    build(core)
    swapped = swap_copies(other, sibling)
    feat_copy(order[0], peer(order[0])).wait_recv()
    forward_copy(order[0], peer(order[0])).start()
    swapped[0].wait_recv()
    build(other)
    for k in order[1:-1]:
        feat_copy(k, peer(k)).wait_recv()
        forward_copy(k, peer(k)).start()
    swapped[1].wait_recv()
    swapped[2].wait_recv()
    mixed = mix(z)
    feat_copy(1, peer(1)).wait_recv()
    across_copy(across).wait_recv()
    mixed = mixed + mix(partner(z, 1))
    for k in order[:-1]:
        forward_copy(k, 2 * partner(z, k) + other).wait_recv()
        mixed = mixed + mix(partner(z, k))
    mixed_hi = mixed.astype(BF16)
    mixed_lo = (mixed - mixed_hi.astype(F32)).astype(BF16)
    weight = weight_ref[...]
    pre_act = (jnp.dot(mixed_hi, weight, preferred_element_type=F32)
               + jnp.dot(mixed_lo, weight, preferred_element_type=F32))
    sig_val = jax.nn.sigmoid(pre_act)
    acts[...] = (pre_act * sig_val).astype(BF16).reshape(acts.shape)
    cot = cot_ref[...].reshape(2 * nodes, -1).astype(F32)
    act_grad = (cot * sig_val * (1.0 + pre_act * (1.0 - sig_val))).astype(BF16)

    def weight_copy(k):
        return pltpu.make_async_remote_copy(
            src_ref=wpart.at[peer(k)], dst_ref=wincoming.at[k - 1],
            send_sem=w_send.at[k - 1], recv_sem=w_recv.at[k - 1],
            device_id={"wide": peer(k)}, device_id_type=MESH)

    weight_part = lax.dot_general(
        mixed_hi, act_grad, (((0,), (0,)), ((), ())), preferred_element_type=F32)
    for c in range(wide):
        wpart[c] = weight_part[c * share:(c + 1) * share]
    for k in order:
        weight_copy(k).start()

    back = lax.dot_general(weight, act_grad, (((1,), (1,)), ((), ())), preferred_element_type=F32).astype(BF16)

    def term_copy(k):
        return pltpu.make_async_remote_copy(
            src_ref=terms.at[k - 1], dst_ref=incoming.at[k - 1],
            send_sem=t_send.at[k - 1], recv_sem=t_recv.at[k - 1],
            device_id={"wide": peer(k)}, device_id_type=MESH)

    for k in order:
        terms[k - 1] = jnp.dot(back, adj[:, rows_of(peer(k))], preferred_element_type=F32).astype(BF16)
        term_copy(k).start()

    own = jnp.dot(back, adj[:, rows_of(me)], preferred_element_type=F32)
    act_ref[0] = acts[core]

    wsum = wpart[me]
    for k in order:
        weight_copy(k).wait_recv()
        wsum = wsum + wincoming[k - 1]
    nbuf[grp] = wsum

    def narrow_copy(j, slot):
        return pltpu.make_async_remote_copy(
            src_ref=nbuf.at[slot], dst_ref=nbuf.at[slot],
            send_sem=n_send.at[j - 1], recv_sem=n_recv.at[j - 1],
            device_id={"narrow": narrow_peer(j)}, device_id_type=MESH)

    for j in range(1, narrow):
        narrow_copy(j, grp).start()

    for k in order:
        term_copy(k).wait_recv()
        own = own + incoming[k - 1].astype(F32)
    fgrad_ref[0] = own.T.astype(BF16)

    for j in range(1, narrow):
        narrow_copy(j, lax.rem(grp - j + narrow, narrow)).wait_recv()
    total = nbuf[0]
    for j in range(1, narrow):
        total = total + nbuf[j]
    wgrad_ref[...] = total

    for copy in swap_copies(core, me) + [across_copy(me)]:
        copy.wait_send()
    for k in order:
        feat_copy(k, me).wait_send()
        if k > 1:
            forward_copy(k, peer(k)).wait_send()
        weight_copy(k).wait_send()
        term_copy(k).wait_send()
    for j in range(1, narrow):
        narrow_copy(j, grp).wait_send()


def hand_over(act_ref, fgrad_ref, wgrad_ref, act_out, fgrad_out, wgrad_out, sems):
    copies = [
        pltpu.make_async_copy(src, dst, sems.at[i])
        for i, (src, dst) in enumerate(((act_ref, act_out), (fgrad_ref, fgrad_out), (wgrad_ref, wgrad_out)))
    ]
    for copy in copies:
        copy.start()
    for copy in copies:
        copy.wait()


def shards(wide, narrow, features, weight, tiles, tile_cols, tile_counts, cotangent):
    _, nodes, width = features.shape
    slots, tile = tiles.shape[2:]
    zs = wide // 2
    if nodes != tile or 2 * zs != wide or zs < 4 or zs & (zs - 1):
        raise ValueError("mesh shape")
    share = width // wide
    vmem = pl.BlockSpec(memory_space=pltpu.VMEM)
    hbm = pl.BlockSpec(memory_space=pltpu.HBM)
    dma = pltpu.SemaphoreType.DMA
    flops = 2 * nodes * tile * width * (5 * wide + 8)
    results = pl.pallas_call(
        functools.partial(kernel, wide, narrow, slots),
        out_shape=(
            pltpu.VMEM((1, nodes, width), BF16),
            pltpu.VMEM((1, nodes, width), BF16),
            pltpu.VMEM((share, width), F32),
        ),
        in_specs=[hbm] * 6,
        out_specs=(vmem, vmem, vmem),
        scratch_shapes=[
            pltpu.VMEM(tile_cols.shape, jnp.int32),
            pltpu.VMEM(tile_counts.shape, jnp.int32),
            pltpu.VMEM(weight.shape, BF16),
            pltpu.VMEM((2, nodes * slots, tile), BF16),
            pltpu.VMEM((2, nodes, width), BF16),
            pltpu.VMEM((wide * tile, width), BF16),
            pltpu.VMEM((2 * nodes, wide * tile), BF16),
            pltpu.VMEM((2, nodes, width), BF16),
            pltpu.VMEM((zs - 1, width, tile), BF16),
            pltpu.VMEM((zs - 1, width, tile), BF16),
            pltpu.VMEM((wide, share, width), F32),
            pltpu.VMEM((zs - 1, share, width), F32),
            pltpu.VMEM((narrow, share, width), F32),
            dma((6,)),
            dma((zs,)), dma((zs,)),
            dma((zs - 1,)), dma((zs - 1,)),
            dma((3,)), dma((3,)),
            dma((zs - 1,)), dma((zs - 1,)),
            dma((zs - 1,)), dma((zs - 1,)),
            dma((narrow - 1,)), dma((narrow - 1,)),
        ],
        compiler_params=pltpu.CompilerParams(
            collective_id=0, has_side_effects=True, vmem_limit_bytes=VMEM_LIMIT),
        cost_estimate=pl.CostEstimate(
            flops=flops, bytes_accessed=2 * nodes * width * (slots + 4), transcendentals=2 * nodes * width),
        name="graph_layer",
    )(*(pltpu.with_memory_space_constraint(x, pltpu.HBM) for x in (
        tile_cols, tile_counts, features, weight, tiles.reshape(nodes * slots, tile), cotangent)))
    return pl.pallas_call(
        hand_over,
        out_shape=tuple(jax.ShapeDtypeStruct(r.shape, r.dtype) for r in results),
        in_specs=[vmem] * 3,
        out_specs=(hbm,) * 3,
        scratch_shapes=[dma((3,))],
        name="hand_over",
    )(*results)


def solution(mesh):
    placed = (
        P("narrow", "wide", None),
        P(),
        P("narrow", "wide", None, None),
        P("narrow", None, None),
        P("narrow", None),
        P("narrow", "wide", None),
    )
    return jax.shard_map(
        functools.partial(shards, mesh.shape["wide"], mesh.shape["narrow"]),
        mesh=mesh,
        in_specs=placed,
        out_specs=(P("narrow", "wide", None), P("narrow", "wide", None), P("wide", None)),
        check_vma=False,
    )
```

```python
import functools

import jax
import jax.numpy as jnp
from jax import lax
from jax.experimental import pallas as pl
from jax.experimental.pallas import tpu as pltpu
from jax.sharding import PartitionSpec as P

MESH = pl.DeviceIdType.MESH
F32 = jnp.float32
BF16 = jnp.bfloat16
VMEM_LIMIT = 32 * 1024 * 1024


def selection(cols_ref, counts_ref, row_block, blocks, slots, chunk):
    shape = (blocks * chunk, chunk * slots)
    row = lax.broadcasted_iota(jnp.int32, shape, 0)
    lane = lax.broadcasted_iota(jnp.int32, (1, chunk * slots), 1)
    slot = lax.rem(lane, slots)
    node = lane // slots
    counts = counts_ref[...]
    here = lax.broadcasted_iota(jnp.int32, counts.shape, 1) == row_block
    count = jnp.sum(jnp.where(here, counts, 0), axis=1, keepdims=True)
    cols = cols_ref[0, pl.ds(row_block, 1), :]
    wanted = jnp.zeros((1, chunk * slots), jnp.int32)
    for s in range(slots):
        wanted = jnp.where(slot == s, cols[:, s:s + 1], wanted)
    wanted = jnp.where(slot < count, wanted * chunk + node, -1)
    return jnp.where(row == wanted, 1.0, 0.0).astype(BF16)


def partner(z, k):
    bit, out = 1, z
    while bit <= k:
        if k & bit:
            out = out + bit - 2 * bit * lax.rem(z // bit, 2)
        bit *= 2
    return out


def partner_order(count):
    order, half = [], count // 2
    while half:
        order += list(range(half, 2 * half))
        half //= 2
    return order


def kernel(
    wide, narrow, slots,
    cols_hbm, counts_hbm, feat_hbm, weight_hbm, tiles_hbm, cot_hbm,
    act_ref, fgrad_ref, wgrad_ref,
    cols_ref, counts_ref, weight_ref, tiles_ref, cot_ref, gathered, adj, acts, terms, incoming, wpart, wincoming, nbuf,
    in_sems, f_send, f_recv, x_send, x_recv, s_send, s_recv, t_send, t_recv, w_send, w_recv, n_send, n_recv,
):
    me = lax.axis_index("wide")
    grp = lax.axis_index("narrow")
    zs = wide // 2
    z, core = me // 2, lax.rem(me, 2)
    other = 1 - core
    sibling = 2 * z + other
    across = 2 * partner(z, 1) + other
    nodes = feat_hbm.shape[1]
    tile = tiles_hbm.shape[1]
    chunk = tile // slots
    share = wgrad_ref.shape[0]
    order = partner_order(zs)

    def peer(k):
        return 2 * partner(z, k) + core

    def narrow_peer(j):
        return lax.rem(grp + j, narrow)

    barrier = pltpu.get_barrier_semaphore()
    for k in order:
        pl.semaphore_signal(barrier, inc=1, device_id={"wide": peer(k)}, device_id_type=MESH)
    for device in (sibling, across):
        pl.semaphore_signal(barrier, inc=1, device_id={"wide": device}, device_id_type=MESH)
    for j in range(1, narrow):
        pl.semaphore_signal(barrier, inc=1, device_id={"narrow": narrow_peer(j)}, device_id_type=MESH)

    def rows_of(index):
        return pl.ds(pl.multiple_of(index * tile, tile), tile)

    loads = [
        pltpu.make_async_copy(src, dst, in_sems.at[i])
        for i, (src, dst) in enumerate((
            (cols_hbm, cols_ref), (counts_hbm, counts_ref), (tiles_hbm, tiles_ref.at[core]),
            (feat_hbm.at[0], gathered.at[rows_of(me)]), (weight_hbm, weight_ref),
            (cot_hbm.at[0], cot_ref.at[core])))
    ]
    for load in loads:
        load.start()
    pl.semaphore_wait(barrier, zs + narrow)

    def feat_copy(k, slot):
        return pltpu.make_async_remote_copy(
            src_ref=feat_hbm.at[0], dst_ref=gathered.at[rows_of(slot)],
            send_sem=f_send.at[k - 1], recv_sem=f_recv.at[k - 1],
            device_id={"wide": peer(k)}, device_id_type=MESH)

    def across_copy(slot):
        return pltpu.make_async_remote_copy(
            src_ref=feat_hbm.at[0], dst_ref=gathered.at[rows_of(slot)],
            send_sem=f_send.at[zs - 1], recv_sem=f_recv.at[zs - 1],
            device_id={"wide": across}, device_id_type=MESH)

    def forward_copy(k, slot):
        return pltpu.make_async_remote_copy(
            src_ref=gathered.at[rows_of(slot)], dst_ref=gathered.at[rows_of(slot)],
            send_sem=x_send.at[k - 1], recv_sem=x_recv.at[k - 1],
            device_id={"wide": sibling}, device_id_type=MESH)

    def swap_copies(half, slot):
        pairs = ((tiles_hbm, tiles_ref.at[half]), (feat_hbm.at[0], gathered.at[rows_of(slot)]),
                 (cot_hbm.at[0], cot_ref.at[half]))
        return [
            pltpu.make_async_remote_copy(
                src_ref=src, dst_ref=dst, send_sem=s_send.at[i], recv_sem=s_recv.at[i],
                device_id={"wide": sibling}, device_id_type=MESH)
            for i, (src, dst) in enumerate(pairs)
        ]

    for k in order:
        feat_copy(k, me).start()
    across_copy(me).start()
    for copy in swap_copies(core, me):
        copy.start()
    for load in loads:
        load.wait()

    def build(half):
        pick = selection(cols_ref, counts_ref, 2 * z + half, wide, slots, chunk)
        base = half * nodes
        for j in range(nodes // chunk):
            part = jnp.dot(
                pick, tiles_ref[half, j * tile:(j + 1) * tile, :], preferred_element_type=F32).astype(BF16)
            rows = pl.ds(pl.multiple_of(base + j * chunk, chunk), chunk)
            for c in range(wide):
                adj[rows, c * tile:(c + 1) * tile] = part[c * chunk:(c + 1) * chunk]

    def mix(chip):
        span = pl.ds(pl.multiple_of(chip * 2 * tile, 2 * tile), 2 * tile)
        return jnp.dot(adj[:, span], gathered[span, :], preferred_element_type=F32)

    build(core)
    swapped = swap_copies(other, sibling)
    feat_copy(order[0], peer(order[0])).wait_recv()
    forward_copy(order[0], peer(order[0])).start()
    swapped[0].wait_recv()
    build(other)
    for k in order[1:-1]:
        feat_copy(k, peer(k)).wait_recv()
        forward_copy(k, peer(k)).start()
    swapped[1].wait_recv()
    swapped[2].wait_recv()
    mixed = mix(z)
    feat_copy(1, peer(1)).wait_recv()
    across_copy(across).wait_recv()
    mixed = mixed + mix(partner(z, 1))
    for k in order[:-1]:
        forward_copy(k, 2 * partner(z, k) + other).wait_recv()
        mixed = mixed + mix(partner(z, k))
    mixed_hi = mixed.astype(BF16)
    mixed_lo = (mixed - mixed_hi.astype(F32)).astype(BF16)
    weight = weight_ref[...]
    pre_act = jnp.dot(
        jnp.concatenate([mixed_hi, mixed_lo], axis=1), jnp.concatenate([weight, weight], axis=0),
        preferred_element_type=F32)
    sig_val = jax.nn.sigmoid(pre_act)
    acts[...] = (pre_act * sig_val).astype(BF16).reshape(acts.shape)
    cot = cot_ref[...].reshape(2 * nodes, -1).astype(F32)
    act_grad = (cot * sig_val * (1.0 + pre_act * (1.0 - sig_val))).astype(BF16)

    def weight_copy(k):
        return pltpu.make_async_remote_copy(
            src_ref=wpart.at[peer(k)], dst_ref=wincoming.at[k - 1],
            send_sem=w_send.at[k - 1], recv_sem=w_recv.at[k - 1],
            device_id={"wide": peer(k)}, device_id_type=MESH)

    weight_part = lax.dot_general(
        mixed_hi, act_grad, (((0,), (0,)), ((), ())), preferred_element_type=F32)
    for c in range(wide):
        wpart[c] = weight_part[c * share:(c + 1) * share]
    for k in order:
        weight_copy(k).start()

    back = lax.dot_general(weight, act_grad, (((1,), (1,)), ((), ())), preferred_element_type=F32).astype(BF16)

    def term_copy(k):
        return pltpu.make_async_remote_copy(
            src_ref=terms.at[k - 1], dst_ref=incoming.at[k - 1],
            send_sem=t_send.at[k - 1], recv_sem=t_recv.at[k - 1],
            device_id={"wide": peer(k)}, device_id_type=MESH)

    for k in order:
        terms[k - 1] = jnp.dot(back, adj[:, rows_of(peer(k))], preferred_element_type=F32).astype(BF16)
        term_copy(k).start()

    own = jnp.dot(back, adj[:, rows_of(me)], preferred_element_type=F32)
    act_ref[0] = acts[core]

    wsum = wpart[me]
    for k in order:
        weight_copy(k).wait_recv()
        wsum = wsum + wincoming[k - 1]
    nbuf[grp] = wsum

    def narrow_copy(j, slot):
        return pltpu.make_async_remote_copy(
            src_ref=nbuf.at[slot], dst_ref=nbuf.at[slot],
            send_sem=n_send.at[j - 1], recv_sem=n_recv.at[j - 1],
            device_id={"narrow": narrow_peer(j)}, device_id_type=MESH)

    for j in range(1, narrow):
        narrow_copy(j, grp).start()

    for k in order:
        term_copy(k).wait_recv()
        own = own + incoming[k - 1].astype(F32)
    fgrad_ref[0] = own.T.astype(BF16)

    for j in range(1, narrow):
        narrow_copy(j, lax.rem(grp - j + narrow, narrow)).wait_recv()
    total = nbuf[0]
    for j in range(1, narrow):
        total = total + nbuf[j]
    wgrad_ref[...] = total

    for copy in swap_copies(core, me) + [across_copy(me)]:
        copy.wait_send()
    for k in order:
        feat_copy(k, me).wait_send()
        if k > 1:
            forward_copy(k, peer(k)).wait_send()
        weight_copy(k).wait_send()
        term_copy(k).wait_send()
    for j in range(1, narrow):
        narrow_copy(j, grp).wait_send()


def hand_over(act_ref, fgrad_ref, wgrad_ref, act_out, fgrad_out, wgrad_out, sems):
    copies = [
        pltpu.make_async_copy(src, dst, sems.at[i])
        for i, (src, dst) in enumerate(((act_ref, act_out), (fgrad_ref, fgrad_out), (wgrad_ref, wgrad_out)))
    ]
    for copy in copies:
        copy.start()
    for copy in copies:
        copy.wait()


def shards(wide, narrow, features, weight, tiles, tile_cols, tile_counts, cotangent):
    _, nodes, width = features.shape
    slots, tile = tiles.shape[2:]
    zs = wide // 2
    if nodes != tile or 2 * zs != wide or zs < 4 or zs & (zs - 1):
        raise ValueError("mesh shape")
    share = width // wide
    vmem = pl.BlockSpec(memory_space=pltpu.VMEM)
    hbm = pl.BlockSpec(memory_space=pltpu.HBM)
    dma = pltpu.SemaphoreType.DMA
    flops = 2 * nodes * tile * width * (5 * wide + 8)
    results = pl.pallas_call(
        functools.partial(kernel, wide, narrow, slots),
        out_shape=(
            pltpu.VMEM((1, nodes, width), BF16),
            pltpu.VMEM((1, nodes, width), BF16),
            pltpu.VMEM((share, width), F32),
        ),
        in_specs=[hbm] * 6,
        out_specs=(vmem, vmem, vmem),
        scratch_shapes=[
            pltpu.VMEM(tile_cols.shape, jnp.int32),
            pltpu.VMEM(tile_counts.shape, jnp.int32),
            pltpu.VMEM(weight.shape, BF16),
            pltpu.VMEM((2, nodes * slots, tile), BF16),
            pltpu.VMEM((2, nodes, width), BF16),
            pltpu.VMEM((wide * tile, width), BF16),
            pltpu.VMEM((2 * nodes, wide * tile), BF16),
            pltpu.VMEM((2, nodes, width), BF16),
            pltpu.VMEM((zs - 1, width, tile), BF16),
            pltpu.VMEM((zs - 1, width, tile), BF16),
            pltpu.VMEM((wide, share, width), F32),
            pltpu.VMEM((zs - 1, share, width), F32),
            pltpu.VMEM((narrow, share, width), F32),
            dma((6,)),
            dma((zs,)), dma((zs,)),
            dma((zs - 1,)), dma((zs - 1,)),
            dma((3,)), dma((3,)),
            dma((zs - 1,)), dma((zs - 1,)),
            dma((zs - 1,)), dma((zs - 1,)),
            dma((narrow - 1,)), dma((narrow - 1,)),
        ],
        compiler_params=pltpu.CompilerParams(
            collective_id=0, has_side_effects=True, vmem_limit_bytes=VMEM_LIMIT),
        cost_estimate=pl.CostEstimate(
            flops=flops, bytes_accessed=2 * nodes * width * (slots + 4), transcendentals=2 * nodes * width),
        name="graph_layer",
    )(*(pltpu.with_memory_space_constraint(x, pltpu.HBM) for x in (
        tile_cols, tile_counts, features, weight, tiles.reshape(nodes * slots, tile), cotangent)))
    return pl.pallas_call(
        hand_over,
        out_shape=tuple(jax.ShapeDtypeStruct(r.shape, r.dtype) for r in results),
        in_specs=[vmem] * 3,
        out_specs=(hbm,) * 3,
        scratch_shapes=[dma((3,))],
        compiler_params=pltpu.CompilerParams(vmem_limit_bytes=2 * 1024 * 1024),
        name="hand_over",
    )(*(pltpu.with_memory_space_constraint(r, pltpu.VMEM) for r in results))


def solution(mesh):
    placed = (
        P("narrow", "wide", None),
        P(),
        P("narrow", "wide", None, None),
        P("narrow", None, None),
        P("narrow", None),
        P("narrow", "wide", None),
    )
    return jax.shard_map(
        functools.partial(shards, mesh.shape["wide"], mesh.shape["narrow"]),
        mesh=mesh,
        in_specs=placed,
        out_specs=(P("narrow", "wide", None), P("narrow", "wide", None), P("wide", None)),
        check_vma=False,
    )
```

```python
import functools

import jax
import jax.numpy as jnp
from jax import lax
from jax.experimental import pallas as pl
from jax.experimental.pallas import tpu as pltpu
from jax.sharding import PartitionSpec as P

MESH = pl.DeviceIdType.MESH
F32 = jnp.float32
BF16 = jnp.bfloat16
VMEM_LIMIT = 32 * 1024 * 1024


def selection(cols_ref, counts_ref, row_block, blocks, slots, chunk):
    shape = (blocks * chunk, chunk * slots)
    row = lax.broadcasted_iota(jnp.int32, shape, 0)
    lane = lax.broadcasted_iota(jnp.int32, (1, chunk * slots), 1)
    slot = lax.rem(lane, slots)
    node = lane // slots
    counts = counts_ref[...]
    here = lax.broadcasted_iota(jnp.int32, counts.shape, 1) == row_block
    count = jnp.sum(jnp.where(here, counts, 0), axis=1, keepdims=True)
    cols = cols_ref[0, pl.ds(row_block, 1), :]
    wanted = jnp.zeros((1, chunk * slots), jnp.int32)
    for s in range(slots):
        wanted = jnp.where(slot == s, cols[:, s:s + 1], wanted)
    wanted = jnp.where(slot < count, wanted * chunk + node, -1)
    return jnp.where(row == wanted, 1.0, 0.0).astype(BF16)


def partner(z, k):
    bit, out = 1, z
    while bit <= k:
        if k & bit:
            out = out + bit - 2 * bit * lax.rem(z // bit, 2)
        bit *= 2
    return out


def partner_order(count):
    order, half = [], count // 2
    while half:
        order += list(range(half, 2 * half))
        half //= 2
    return order


def kernel(
    wide, narrow, slots,
    cols_hbm, counts_hbm, feat_hbm, weight_hbm, tiles_hbm, cot_hbm,
    act_ref, fgrad_ref, wgrad_ref,
    cols_ref, counts_ref, weight_ref, tiles_ref, cot_ref, gathered, adj, acts, terms, incoming, wpart, wincoming, nbuf,
    in_sems, f_send, f_recv, x_send, x_recv, s_send, s_recv, t_send, t_recv, w_send, w_recv, n_send, n_recv,
):
    me = lax.axis_index("wide")
    grp = lax.axis_index("narrow")
    zs = wide // 2
    z, core = me // 2, lax.rem(me, 2)
    other = 1 - core
    sibling = 2 * z + other
    across = 2 * partner(z, 1) + other
    nodes = feat_hbm.shape[1]
    tile = tiles_hbm.shape[1]
    chunk = tile // slots
    share = wgrad_ref.shape[0]
    order = partner_order(zs)

    def peer(k):
        return 2 * partner(z, k) + core

    def narrow_peer(j):
        return lax.rem(grp + j, narrow)

    barrier = pltpu.get_barrier_semaphore()
    for k in order:
        pl.semaphore_signal(barrier, inc=1, device_id={"wide": peer(k)}, device_id_type=MESH)
    for device in (sibling, across):
        pl.semaphore_signal(barrier, inc=1, device_id={"wide": device}, device_id_type=MESH)
    for j in range(1, narrow):
        pl.semaphore_signal(barrier, inc=1, device_id={"narrow": narrow_peer(j)}, device_id_type=MESH)

    def rows_of(index):
        return pl.ds(pl.multiple_of(index * tile, tile), tile)

    loads = [
        pltpu.make_async_copy(src, dst, in_sems.at[i])
        for i, (src, dst) in enumerate((
            (cols_hbm, cols_ref), (counts_hbm, counts_ref), (tiles_hbm, tiles_ref.at[core]),
            (feat_hbm.at[0], gathered.at[rows_of(me)]), (weight_hbm, weight_ref),
            (cot_hbm.at[0], cot_ref.at[core])))
    ]
    pl.semaphore_wait(barrier, zs + narrow)

    def feat_copy(k, slot):
        return pltpu.make_async_remote_copy(
            src_ref=feat_hbm.at[0], dst_ref=gathered.at[rows_of(slot)],
            send_sem=f_send.at[k - 1], recv_sem=f_recv.at[k - 1],
            device_id={"wide": peer(k)}, device_id_type=MESH)

    def across_copy(slot):
        return pltpu.make_async_remote_copy(
            src_ref=feat_hbm.at[0], dst_ref=gathered.at[rows_of(slot)],
            send_sem=f_send.at[zs - 1], recv_sem=f_recv.at[zs - 1],
            device_id={"wide": across}, device_id_type=MESH)

    def forward_copy(k, slot):
        return pltpu.make_async_remote_copy(
            src_ref=gathered.at[rows_of(slot)], dst_ref=gathered.at[rows_of(slot)],
            send_sem=x_send.at[k - 1], recv_sem=x_recv.at[k - 1],
            device_id={"wide": sibling}, device_id_type=MESH)

    def swap_copies(half, slot):
        pairs = ((tiles_hbm, tiles_ref.at[half]), (feat_hbm.at[0], gathered.at[rows_of(slot)]),
                 (cot_hbm.at[0], cot_ref.at[half]))
        return [
            pltpu.make_async_remote_copy(
                src_ref=src, dst_ref=dst, send_sem=s_send.at[i], recv_sem=s_recv.at[i],
                device_id={"wide": sibling}, device_id_type=MESH)
            for i, (src, dst) in enumerate(pairs)
        ]

    for k in order:
        feat_copy(k, me).start()
    across_copy(me).start()
    for copy in swap_copies(core, me):
        copy.start()
    for load in loads:
        load.start()
    for load in loads:
        load.wait()

    def build(half):
        pick = selection(cols_ref, counts_ref, 2 * z + half, wide, slots, chunk)
        base = half * nodes
        for j in range(nodes // chunk):
            part = jnp.dot(
                pick, tiles_ref[half, j * tile:(j + 1) * tile, :], preferred_element_type=F32).astype(BF16)
            rows = pl.ds(pl.multiple_of(base + j * chunk, chunk), chunk)
            for c in range(wide):
                adj[rows, c * tile:(c + 1) * tile] = part[c * chunk:(c + 1) * chunk]

    def mix(chip):
        span = pl.ds(pl.multiple_of(chip * 2 * tile, 2 * tile), 2 * tile)
        return jnp.dot(adj[:, span], gathered[span, :], preferred_element_type=F32)

    build(core)
    swapped = swap_copies(other, sibling)
    feat_copy(order[0], peer(order[0])).wait_recv()
    forward_copy(order[0], peer(order[0])).start()
    swapped[0].wait_recv()
    build(other)
    for k in order[1:-1]:
        feat_copy(k, peer(k)).wait_recv()
        forward_copy(k, peer(k)).start()
    swapped[1].wait_recv()
    swapped[2].wait_recv()
    mixed = mix(z)
    feat_copy(1, peer(1)).wait_recv()
    across_copy(across).wait_recv()
    mixed = mixed + mix(partner(z, 1))
    for k in order[:-1]:
        forward_copy(k, 2 * partner(z, k) + other).wait_recv()
        mixed = mixed + mix(partner(z, k))
    mixed_hi = mixed.astype(BF16)
    mixed_lo = (mixed - mixed_hi.astype(F32)).astype(BF16)
    weight = weight_ref[...]
    pre_act = jnp.dot(
        jnp.concatenate([mixed_hi, mixed_lo], axis=1), jnp.concatenate([weight, weight], axis=0),
        preferred_element_type=F32)
    sig_val = jax.nn.sigmoid(pre_act)
    acts[...] = (pre_act * sig_val).astype(BF16).reshape(acts.shape)
    cot = cot_ref[...].reshape(2 * nodes, -1).astype(F32)
    act_grad = (cot * sig_val * (1.0 + pre_act * (1.0 - sig_val))).astype(BF16)

    def weight_copy(k):
        return pltpu.make_async_remote_copy(
            src_ref=wpart.at[peer(k)], dst_ref=wincoming.at[k - 1],
            send_sem=w_send.at[k - 1], recv_sem=w_recv.at[k - 1],
            device_id={"wide": peer(k)}, device_id_type=MESH)

    back = lax.dot_general(weight, act_grad, (((1,), (1,)), ((), ())), preferred_element_type=F32).astype(BF16)

    def term_copy(k):
        return pltpu.make_async_remote_copy(
            src_ref=terms.at[k - 1], dst_ref=incoming.at[k - 1],
            send_sem=t_send.at[k - 1], recv_sem=t_recv.at[k - 1],
            device_id={"wide": peer(k)}, device_id_type=MESH)

    def send_term(k):
        terms[k - 1] = jnp.dot(back, adj[:, rows_of(peer(k))], preferred_element_type=F32).astype(BF16)
        term_copy(k).start()

    send_term(order[0])
    weight_part = lax.dot_general(
        mixed_hi, act_grad, (((0,), (0,)), ((), ())), preferred_element_type=F32)
    for c in range(wide):
        wpart[c] = weight_part[c * share:(c + 1) * share]
    for k in order:
        weight_copy(k).start()

    for k in order[1:]:
        send_term(k)

    own = jnp.dot(back, adj[:, rows_of(me)], preferred_element_type=F32)
    act_ref[0] = acts[core]

    wsum = wpart[me]
    for k in order:
        weight_copy(k).wait_recv()
        wsum = wsum + wincoming[k - 1]
    nbuf[grp] = wsum

    def narrow_copy(j, slot):
        return pltpu.make_async_remote_copy(
            src_ref=nbuf.at[slot], dst_ref=nbuf.at[slot],
            send_sem=n_send.at[j - 1], recv_sem=n_recv.at[j - 1],
            device_id={"narrow": narrow_peer(j)}, device_id_type=MESH)

    for j in range(1, narrow):
        narrow_copy(j, grp).start()

    for k in order:
        term_copy(k).wait_recv()
        own = own + incoming[k - 1].astype(F32)
    fgrad_ref[0] = own.T.astype(BF16)

    for j in range(1, narrow):
        narrow_copy(j, lax.rem(grp - j + narrow, narrow)).wait_recv()
    total = nbuf[0]
    for j in range(1, narrow):
        total = total + nbuf[j]
    wgrad_ref[...] = total

    for copy in swap_copies(core, me) + [across_copy(me)]:
        copy.wait_send()
    for k in order:
        feat_copy(k, me).wait_send()
        if k > 1:
            forward_copy(k, peer(k)).wait_send()
        weight_copy(k).wait_send()
        term_copy(k).wait_send()
    for j in range(1, narrow):
        narrow_copy(j, grp).wait_send()


def hand_over(act_ref, fgrad_ref, wgrad_ref, act_out, fgrad_out, wgrad_out, sems):
    copies = [
        pltpu.make_async_copy(src, dst, sems.at[i])
        for i, (src, dst) in enumerate(((act_ref, act_out), (fgrad_ref, fgrad_out), (wgrad_ref, wgrad_out)))
    ]
    for copy in copies:
        copy.start()
    for copy in copies:
        copy.wait()


def shards(wide, narrow, features, weight, tiles, tile_cols, tile_counts, cotangent):
    _, nodes, width = features.shape
    slots, tile = tiles.shape[2:]
    zs = wide // 2
    if nodes != tile or 2 * zs != wide or zs < 4 or zs & (zs - 1):
        raise ValueError("mesh shape")
    share = width // wide
    vmem = pl.BlockSpec(memory_space=pltpu.VMEM)
    hbm = pl.BlockSpec(memory_space=pltpu.HBM)
    dma = pltpu.SemaphoreType.DMA
    flops = 2 * nodes * tile * width * (5 * wide + 8)
    results = pl.pallas_call(
        functools.partial(kernel, wide, narrow, slots),
        out_shape=(
            pltpu.VMEM((1, nodes, width), BF16),
            pltpu.VMEM((1, nodes, width), BF16),
            pltpu.VMEM((share, width), F32),
        ),
        in_specs=[hbm] * 6,
        out_specs=(vmem, vmem, vmem),
        scratch_shapes=[
            pltpu.VMEM(tile_cols.shape, jnp.int32),
            pltpu.VMEM(tile_counts.shape, jnp.int32),
            pltpu.VMEM(weight.shape, BF16),
            pltpu.VMEM((2, nodes * slots, tile), BF16),
            pltpu.VMEM((2, nodes, width), BF16),
            pltpu.VMEM((wide * tile, width), BF16),
            pltpu.VMEM((2 * nodes, wide * tile), BF16),
            pltpu.VMEM((2, nodes, width), BF16),
            pltpu.VMEM((zs - 1, width, tile), BF16),
            pltpu.VMEM((zs - 1, width, tile), BF16),
            pltpu.VMEM((wide, share, width), F32),
            pltpu.VMEM((zs - 1, share, width), F32),
            pltpu.VMEM((narrow, share, width), F32),
            dma((6,)),
            dma((zs,)), dma((zs,)),
            dma((zs - 1,)), dma((zs - 1,)),
            dma((3,)), dma((3,)),
            dma((zs - 1,)), dma((zs - 1,)),
            dma((zs - 1,)), dma((zs - 1,)),
            dma((narrow - 1,)), dma((narrow - 1,)),
        ],
        compiler_params=pltpu.CompilerParams(
            collective_id=0, has_side_effects=True, vmem_limit_bytes=VMEM_LIMIT),
        cost_estimate=pl.CostEstimate(
            flops=flops, bytes_accessed=2 * nodes * width * (slots + 4), transcendentals=2 * nodes * width),
        name="graph_layer",
    )(*(pltpu.with_memory_space_constraint(x, pltpu.HBM) for x in (
        tile_cols, tile_counts, features, weight, tiles.reshape(nodes * slots, tile), cotangent)))
    return pl.pallas_call(
        hand_over,
        out_shape=tuple(jax.ShapeDtypeStruct(r.shape, r.dtype) for r in results),
        in_specs=[vmem] * 3,
        out_specs=(hbm,) * 3,
        scratch_shapes=[dma((3,))],
        compiler_params=pltpu.CompilerParams(vmem_limit_bytes=2 * 1024 * 1024),
        name="hand_over",
    )(*(pltpu.with_memory_space_constraint(r, pltpu.VMEM) for r in results))


def solution(mesh):
    placed = (
        P("narrow", "wide", None),
        P(),
        P("narrow", "wide", None, None),
        P("narrow", None, None),
        P("narrow", None),
        P("narrow", "wide", None),
    )
    return jax.shard_map(
        functools.partial(shards, mesh.shape["wide"], mesh.shape["narrow"]),
        mesh=mesh,
        in_specs=placed,
        out_specs=(P("narrow", "wide", None), P("narrow", "wide", None), P("wide", None)),
        check_vma=False,
    )
```

```python
import functools

import jax
import jax.numpy as jnp
from jax import lax
from jax.experimental import pallas as pl
from jax.experimental.pallas import tpu as pltpu
from jax.sharding import PartitionSpec as P

MESH = pl.DeviceIdType.MESH
F32 = jnp.float32
BF16 = jnp.bfloat16
VMEM_LIMIT = 32 * 1024 * 1024


def selection(cols_ref, counts_ref, row_block, blocks, slots, chunk):
    shape = (blocks * chunk, chunk * slots)
    row = lax.broadcasted_iota(jnp.int32, shape, 0)
    lane = lax.broadcasted_iota(jnp.int32, (1, chunk * slots), 1)
    slot = lax.rem(lane, slots)
    node = lane // slots
    counts = counts_ref[...]
    here = lax.broadcasted_iota(jnp.int32, counts.shape, 1) == row_block
    count = jnp.sum(jnp.where(here, counts, 0), axis=1, keepdims=True)
    cols = cols_ref[0, pl.ds(row_block, 1), :]
    wanted = jnp.zeros((1, chunk * slots), jnp.int32)
    for s in range(slots):
        wanted = jnp.where(slot == s, cols[:, s:s + 1], wanted)
    wanted = jnp.where(slot < count, wanted * chunk + node, -1)
    return jnp.where(row == wanted, 1.0, 0.0).astype(BF16)


def partner(z, k):
    bit, out = 1, z
    while bit <= k:
        if k & bit:
            out = out + bit - 2 * bit * lax.rem(z // bit, 2)
        bit *= 2
    return out


def partner_order(count):
    order, half = [], count // 2
    while half:
        order += list(range(half, 2 * half))
        half //= 2
    return order


def kernel(
    wide, narrow, slots,
    cols_hbm, counts_hbm, feat_hbm, weight_hbm, tiles_hbm, cot_hbm,
    act_ref, fgrad_ref, wgrad_ref,
    cols_ref, counts_ref, weight_ref, tiles_ref, cot_ref, gathered, adj, acts, terms, incoming, wpart, wincoming, nbuf,
    in_sems, f_send, f_recv, x_send, x_recv, s_send, s_recv, t_send, t_recv, w_send, w_recv, n_send, n_recv,
):
    me = lax.axis_index("wide")
    grp = lax.axis_index("narrow")
    zs = wide // 2
    z, core = me // 2, lax.rem(me, 2)
    other = 1 - core
    sibling = 2 * z + other
    across = 2 * partner(z, 1) + other
    nodes = feat_hbm.shape[1]
    tile = tiles_hbm.shape[1]
    chunk = tile // slots
    share = wgrad_ref.shape[0]
    order = partner_order(zs)

    def peer(k):
        return 2 * partner(z, k) + core

    def narrow_peer(j):
        return lax.rem(grp + j, narrow)

    barrier = pltpu.get_barrier_semaphore()
    for k in order:
        pl.semaphore_signal(barrier, inc=1, device_id={"wide": peer(k)}, device_id_type=MESH)
    for device in (sibling, across):
        pl.semaphore_signal(barrier, inc=1, device_id={"wide": device}, device_id_type=MESH)
    for j in range(1, narrow):
        pl.semaphore_signal(barrier, inc=1, device_id={"narrow": narrow_peer(j)}, device_id_type=MESH)

    def rows_of(index):
        return pl.ds(pl.multiple_of(index * tile, tile), tile)

    loads = [
        pltpu.make_async_copy(src, dst, in_sems.at[i])
        for i, (src, dst) in enumerate((
            (cols_hbm, cols_ref), (counts_hbm, counts_ref), (tiles_hbm, tiles_ref.at[core]),
            (feat_hbm.at[0], gathered.at[rows_of(me)]), (weight_hbm, weight_ref),
            (cot_hbm.at[0], cot_ref.at[core])))
    ]
    for load in loads:
        load.start()
    pl.semaphore_wait(barrier, zs + narrow)

    def feat_copy(k, slot):
        return pltpu.make_async_remote_copy(
            src_ref=feat_hbm.at[0], dst_ref=gathered.at[rows_of(slot)],
            send_sem=f_send.at[k - 1], recv_sem=f_recv.at[k - 1],
            device_id={"wide": peer(k)}, device_id_type=MESH)

    def across_copy(slot):
        return pltpu.make_async_remote_copy(
            src_ref=feat_hbm.at[0], dst_ref=gathered.at[rows_of(slot)],
            send_sem=f_send.at[zs - 1], recv_sem=f_recv.at[zs - 1],
            device_id={"wide": across}, device_id_type=MESH)

    def forward_copy(k, slot):
        return pltpu.make_async_remote_copy(
            src_ref=gathered.at[rows_of(slot)], dst_ref=gathered.at[rows_of(slot)],
            send_sem=x_send.at[k - 1], recv_sem=x_recv.at[k - 1],
            device_id={"wide": sibling}, device_id_type=MESH)

    def swap_copies(half, slot):
        piece = nodes * slots // 2
        pairs = [(tiles_hbm.at[pl.ds(i * piece, piece)], tiles_ref.at[half, pl.ds(i * piece, piece)]) for i in range(2)]
        pairs += [(feat_hbm.at[0], gathered.at[rows_of(slot)]), (cot_hbm.at[0], cot_ref.at[half])]
        return [
            pltpu.make_async_remote_copy(
                src_ref=src, dst_ref=dst, send_sem=s_send.at[i], recv_sem=s_recv.at[i],
                device_id={"wide": sibling}, device_id_type=MESH)
            for i, (src, dst) in enumerate(pairs)
        ]

    outgoing = swap_copies(core, me)
    for k in order[:-1]:
        feat_copy(k, me).start()
    outgoing[0].start()
    outgoing[1].start()
    feat_copy(1, me).start()
    across_copy(me).start()
    outgoing[2].start()
    outgoing[3].start()
    for load in loads[:3]:
        load.wait()

    def build(half, pick, piece):
        count = nodes // chunk // 2
        for j in range(piece * count, (piece + 1) * count, 2):
            both = jnp.concatenate(
                [tiles_ref[half, i * tile:(i + 1) * tile, :] for i in (j, j + 1)], axis=1)
            part = jnp.dot(pick, both, preferred_element_type=F32).astype(BF16)
            for i in range(2):
                rows = pl.ds(pl.multiple_of(half * nodes + (j + i) * chunk, chunk), chunk)
                for c in range(wide):
                    adj[rows, c * tile:(c + 1) * tile] = part[
                        c * chunk:(c + 1) * chunk, i * tile:(i + 1) * tile]

    def mix(chip):
        span = pl.ds(pl.multiple_of(chip * 2 * tile, 2 * tile), 2 * tile)
        return jnp.dot(adj[:, span], gathered[span, :], preferred_element_type=F32)

    pick = selection(cols_ref, counts_ref, 2 * z + core, wide, slots, chunk)
    build(core, pick, 0)
    build(core, pick, 1)
    pick = selection(cols_ref, counts_ref, 2 * z + other, wide, slots, chunk)
    swapped = swap_copies(other, sibling)
    feat_copy(order[0], peer(order[0])).wait_recv()
    forward_copy(order[0], peer(order[0])).start()
    for piece in range(2):
        swapped[piece].wait_recv()
        build(other, pick, piece)
    for k in order[1:-1]:
        feat_copy(k, peer(k)).wait_recv()
        forward_copy(k, peer(k)).start()
    for load in loads[3:]:
        load.wait()
    swapped[2].wait_recv()
    swapped[3].wait_recv()
    mixed = mix(z)
    feat_copy(1, peer(1)).wait_recv()
    across_copy(across).wait_recv()
    mixed = mixed + mix(partner(z, 1))
    for k in order[:-1]:
        forward_copy(k, 2 * partner(z, k) + other).wait_recv()
        mixed = mixed + mix(partner(z, k))
    mixed_hi = mixed.astype(BF16)
    mixed_lo = (mixed - mixed_hi.astype(F32)).astype(BF16)
    weight = weight_ref[...]
    pre_act = jnp.dot(
        jnp.concatenate([mixed_hi, mixed_lo], axis=1), jnp.concatenate([weight, weight], axis=0),
        preferred_element_type=F32)
    sig_val = jax.nn.sigmoid(pre_act)
    acts[...] = (pre_act * sig_val).astype(BF16).reshape(acts.shape)
    cot = cot_ref[...].reshape(2 * nodes, -1).astype(F32)
    act_grad = (cot * sig_val * (1.0 + pre_act * (1.0 - sig_val))).astype(BF16)

    def weight_copy(k):
        return pltpu.make_async_remote_copy(
            src_ref=wpart.at[peer(k)], dst_ref=wincoming.at[k - 1],
            send_sem=w_send.at[k - 1], recv_sem=w_recv.at[k - 1],
            device_id={"wide": peer(k)}, device_id_type=MESH)

    weight_part = lax.dot_general(
        mixed_hi, act_grad, (((0,), (0,)), ((), ())), preferred_element_type=F32)
    for c in range(wide):
        wpart[c] = weight_part[c * share:(c + 1) * share]
    for k in order:
        weight_copy(k).start()

    back = lax.dot_general(weight, act_grad, (((1,), (1,)), ((), ())), preferred_element_type=F32).astype(BF16)

    def term_copy(k):
        return pltpu.make_async_remote_copy(
            src_ref=terms.at[k - 1], dst_ref=incoming.at[k - 1],
            send_sem=t_send.at[k - 1], recv_sem=t_recv.at[k - 1],
            device_id={"wide": peer(k)}, device_id_type=MESH)

    for k in order:
        terms[k - 1] = jnp.dot(back, adj[:, rows_of(peer(k))], preferred_element_type=F32).astype(BF16)
        term_copy(k).start()

    own = jnp.dot(back, adj[:, rows_of(me)], preferred_element_type=F32)
    act_ref[0] = acts[core]

    wsum = wpart[me]
    for k in order:
        weight_copy(k).wait_recv()
        wsum = wsum + wincoming[k - 1]
    nbuf[grp] = wsum

    def narrow_copy(j, slot):
        return pltpu.make_async_remote_copy(
            src_ref=nbuf.at[slot], dst_ref=nbuf.at[slot],
            send_sem=n_send.at[j - 1], recv_sem=n_recv.at[j - 1],
            device_id={"narrow": narrow_peer(j)}, device_id_type=MESH)

    for j in range(1, narrow):
        narrow_copy(j, grp).start()

    for k in order:
        term_copy(k).wait_recv()
        own = own + incoming[k - 1].astype(F32)
    fgrad_ref[0] = own.T.astype(BF16)

    for j in range(1, narrow):
        narrow_copy(j, lax.rem(grp - j + narrow, narrow)).wait_recv()
    total = nbuf[0]
    for j in range(1, narrow):
        total = total + nbuf[j]
    wgrad_ref[...] = total

    for copy in swap_copies(core, me) + [across_copy(me)]:
        copy.wait_send()
    for k in order:
        feat_copy(k, me).wait_send()
        if k > 1:
            forward_copy(k, peer(k)).wait_send()
        weight_copy(k).wait_send()
        term_copy(k).wait_send()
    for j in range(1, narrow):
        narrow_copy(j, grp).wait_send()


def hand_over(act_ref, fgrad_ref, wgrad_ref, act_out, fgrad_out, wgrad_out, sems):
    copies = [
        pltpu.make_async_copy(src, dst, sems.at[i])
        for i, (src, dst) in enumerate(((act_ref, act_out), (fgrad_ref, fgrad_out), (wgrad_ref, wgrad_out)))
    ]
    for copy in copies:
        copy.start()
    for copy in copies:
        copy.wait()


def shards(wide, narrow, features, weight, tiles, tile_cols, tile_counts, cotangent):
    _, nodes, width = features.shape
    slots, tile = tiles.shape[2:]
    zs = wide // 2
    if nodes != tile or 2 * zs != wide or zs < 4 or zs & (zs - 1):
        raise ValueError("mesh shape")
    share = width // wide
    vmem = pl.BlockSpec(memory_space=pltpu.VMEM)
    hbm = pl.BlockSpec(memory_space=pltpu.HBM)
    dma = pltpu.SemaphoreType.DMA
    flops = 2 * nodes * tile * width * (5 * wide + 8)
    results = pl.pallas_call(
        functools.partial(kernel, wide, narrow, slots),
        out_shape=(
            pltpu.VMEM((1, nodes, width), BF16),
            pltpu.VMEM((1, nodes, width), BF16),
            pltpu.VMEM((share, width), F32),
        ),
        in_specs=[hbm] * 6,
        out_specs=(vmem, vmem, vmem),
        scratch_shapes=[
            pltpu.VMEM(tile_cols.shape, jnp.int32),
            pltpu.VMEM(tile_counts.shape, jnp.int32),
            pltpu.VMEM(weight.shape, BF16),
            pltpu.VMEM((2, nodes * slots, tile), BF16),
            pltpu.VMEM((2, nodes, width), BF16),
            pltpu.VMEM((wide * tile, width), BF16),
            pltpu.VMEM((2 * nodes, wide * tile), BF16),
            pltpu.VMEM((2, nodes, width), BF16),
            pltpu.VMEM((zs - 1, width, tile), BF16),
            pltpu.VMEM((zs - 1, width, tile), BF16),
            pltpu.VMEM((wide, share, width), F32),
            pltpu.VMEM((zs - 1, share, width), F32),
            pltpu.VMEM((narrow, share, width), F32),
            dma((6,)),
            dma((zs,)), dma((zs,)),
            dma((zs - 1,)), dma((zs - 1,)),
            dma((4,)), dma((4,)),
            dma((zs - 1,)), dma((zs - 1,)),
            dma((zs - 1,)), dma((zs - 1,)),
            dma((narrow - 1,)), dma((narrow - 1,)),
        ],
        compiler_params=pltpu.CompilerParams(
            collective_id=0, has_side_effects=True, vmem_limit_bytes=VMEM_LIMIT),
        cost_estimate=pl.CostEstimate(
            flops=flops, bytes_accessed=2 * nodes * width * (slots + 4), transcendentals=2 * nodes * width),
        name="graph_layer",
    )(*(pltpu.with_memory_space_constraint(x, pltpu.HBM) for x in (
        tile_cols, tile_counts, features, weight, tiles.reshape(nodes * slots, tile), cotangent)))
    return pl.pallas_call(
        hand_over,
        out_shape=tuple(jax.ShapeDtypeStruct(r.shape, r.dtype) for r in results),
        in_specs=[vmem] * 3,
        out_specs=(hbm,) * 3,
        scratch_shapes=[dma((3,))],
        compiler_params=pltpu.CompilerParams(vmem_limit_bytes=2 * 1024 * 1024),
        name="hand_over",
    )(*(pltpu.with_memory_space_constraint(r, pltpu.VMEM) for r in results))


def solution(mesh):
    placed = (
        P("narrow", "wide", None),
        P(),
        P("narrow", "wide", None, None),
        P("narrow", None, None),
        P("narrow", None),
        P("narrow", "wide", None),
    )
    return jax.shard_map(
        functools.partial(shards, mesh.shape["wide"], mesh.shape["narrow"]),
        mesh=mesh,
        in_specs=placed,
        out_specs=(P("narrow", "wide", None), P("narrow", "wide", None), P("wide", None)),
        check_vma=False,
    )
```

```python
import functools

import jax
import jax.numpy as jnp
from jax import lax
from jax.experimental import pallas as pl
from jax.experimental.pallas import tpu as pltpu
from jax.sharding import PartitionSpec as P

MESH = pl.DeviceIdType.MESH
F32 = jnp.float32
BF16 = jnp.bfloat16
VMEM_LIMIT = 32 * 1024 * 1024


def selection(cols_ref, counts_ref, row_block, blocks, slots, chunk):
    shape = (blocks * chunk, chunk * slots)
    row = lax.broadcasted_iota(jnp.int32, shape, 0)
    lane = lax.broadcasted_iota(jnp.int32, (1, chunk * slots), 1)
    slot = lax.rem(lane, slots)
    node = lane // slots
    counts = counts_ref[...]
    here = lax.broadcasted_iota(jnp.int32, counts.shape, 1) == row_block
    count = jnp.sum(jnp.where(here, counts, 0), axis=1, keepdims=True)
    cols = cols_ref[0, pl.ds(row_block, 1), :]
    wanted = jnp.zeros((1, chunk * slots), jnp.int32)
    for s in range(slots):
        wanted = jnp.where(slot == s, cols[:, s:s + 1], wanted)
    wanted = jnp.where(slot < count, wanted * chunk + node, -1)
    return jnp.where(row == wanted, 1.0, 0.0).astype(BF16)


def partner(z, k):
    bit, out = 1, z
    while bit <= k:
        if k & bit:
            out = out + bit - 2 * bit * lax.rem(z // bit, 2)
        bit *= 2
    return out


def partner_order(count):
    order, half = [], count // 2
    while half:
        order += list(range(half, 2 * half))
        half //= 2
    return order


def kernel(
    wide, narrow, slots,
    cols_hbm, counts_hbm, feat_hbm, weight_hbm, tiles_hbm, cot_hbm,
    act_ref, fgrad_ref, wgrad_ref,
    cols_ref, counts_ref, weight_ref, tiles_ref, cot_ref, gathered, adj, acts, terms, incoming, wpart, wincoming, nbuf,
    in_sems, f_send, f_recv, x_send, x_recv, s_send, s_recv, t_send, t_recv, w_send, w_recv, n_send, n_recv,
):
    me = lax.axis_index("wide")
    grp = lax.axis_index("narrow")
    zs = wide // 2
    z, core = me // 2, lax.rem(me, 2)
    other = 1 - core
    sibling = 2 * z + other
    across = 2 * partner(z, 1) + other
    nodes = feat_hbm.shape[1]
    tile = tiles_hbm.shape[1]
    chunk = tile // slots
    share = wgrad_ref.shape[0]
    order = partner_order(zs)

    def peer(k):
        return 2 * partner(z, k) + core

    def narrow_peer(j):
        return lax.rem(grp + j, narrow)

    barrier = pltpu.get_barrier_semaphore()
    for k in order:
        pl.semaphore_signal(barrier, inc=1, device_id={"wide": peer(k)}, device_id_type=MESH)
    for device in (sibling, across):
        pl.semaphore_signal(barrier, inc=1, device_id={"wide": device}, device_id_type=MESH)
    for j in range(1, narrow):
        pl.semaphore_signal(barrier, inc=1, device_id={"narrow": narrow_peer(j)}, device_id_type=MESH)

    def rows_of(index):
        return pl.ds(pl.multiple_of(index * tile, tile), tile)

    loads = [
        pltpu.make_async_copy(src, dst, in_sems.at[i])
        for i, (src, dst) in enumerate((
            (cols_hbm, cols_ref), (counts_hbm, counts_ref), (tiles_hbm, tiles_ref.at[core]),
            (feat_hbm.at[0], gathered.at[rows_of(me)]), (weight_hbm, weight_ref),
            (cot_hbm.at[0], cot_ref.at[core])))
    ]
    for load in loads:
        load.start()
    pl.semaphore_wait(barrier, zs + narrow)

    def feat_copy(k, slot):
        return pltpu.make_async_remote_copy(
            src_ref=feat_hbm.at[0], dst_ref=gathered.at[rows_of(slot)],
            send_sem=f_send.at[k - 1], recv_sem=f_recv.at[k - 1],
            device_id={"wide": peer(k)}, device_id_type=MESH)

    def across_copy(slot):
        return pltpu.make_async_remote_copy(
            src_ref=feat_hbm.at[0], dst_ref=gathered.at[rows_of(slot)],
            send_sem=f_send.at[zs - 1], recv_sem=f_recv.at[zs - 1],
            device_id={"wide": across}, device_id_type=MESH)

    def forward_copy(k, slot):
        return pltpu.make_async_remote_copy(
            src_ref=gathered.at[rows_of(slot)], dst_ref=gathered.at[rows_of(slot)],
            send_sem=x_send.at[k - 1], recv_sem=x_recv.at[k - 1],
            device_id={"wide": sibling}, device_id_type=MESH)

    def swap_copies(half, slot):
        piece = nodes * slots // 2
        pairs = [(tiles_hbm.at[pl.ds(i * piece, piece)], tiles_ref.at[half, pl.ds(i * piece, piece)]) for i in range(2)]
        pairs += [(feat_hbm.at[0], gathered.at[rows_of(slot)]), (cot_hbm.at[0], cot_ref.at[half])]
        return [
            pltpu.make_async_remote_copy(
                src_ref=src, dst_ref=dst, send_sem=s_send.at[i], recv_sem=s_recv.at[i],
                device_id={"wide": sibling}, device_id_type=MESH)
            for i, (src, dst) in enumerate(pairs)
        ]

    outgoing = swap_copies(core, me)
    for k in order[:-1]:
        feat_copy(k, me).start()
    outgoing[0].start()
    outgoing[1].start()
    feat_copy(1, me).start()
    across_copy(me).start()
    outgoing[2].start()
    outgoing[3].start()
    for load in loads[:3]:
        load.wait()

    def build(half, pick, piece):
        count = nodes // chunk // 2
        for j in range(piece * count, (piece + 1) * count, 2):
            both = jnp.concatenate(
                [tiles_ref[half, i * tile:(i + 1) * tile, :] for i in (j, j + 1)], axis=1)
            part = jnp.dot(pick, both, preferred_element_type=F32).astype(BF16)
            for i in range(2):
                rows = pl.ds(pl.multiple_of(half * nodes + (j + i) * chunk, chunk), chunk)
                for c in range(wide):
                    adj[rows, c * tile:(c + 1) * tile] = part[
                        c * chunk:(c + 1) * chunk, i * tile:(i + 1) * tile]

    def mix(chip):
        span = pl.ds(pl.multiple_of(chip * 2 * tile, 2 * tile), 2 * tile)
        return jnp.dot(adj[:, span], gathered[span, :], preferred_element_type=F32)

    pick = selection(cols_ref, counts_ref, 2 * z + core, wide, slots, chunk)
    build(core, pick, 0)
    build(core, pick, 1)
    pick = selection(cols_ref, counts_ref, 2 * z + other, wide, slots, chunk)
    swapped = swap_copies(other, sibling)
    feat_copy(order[0], peer(order[0])).wait_recv()
    forward_copy(order[0], peer(order[0])).start()
    for piece in range(2):
        swapped[piece].wait_recv()
        build(other, pick, piece)
    for k in order[1:-1]:
        feat_copy(k, peer(k)).wait_recv()
        forward_copy(k, peer(k)).start()
    for load in loads[3:]:
        load.wait()
    swapped[2].wait_recv()
    swapped[3].wait_recv()
    mixed = mix(z)
    feat_copy(1, peer(1)).wait_recv()
    across_copy(across).wait_recv()
    mixed = mixed + mix(partner(z, 1))
    for k in order[:-1]:
        forward_copy(k, 2 * partner(z, k) + other).wait_recv()
        mixed = mixed + mix(partner(z, k))
    mixed_hi = mixed.astype(BF16)
    mixed_lo = (mixed - mixed_hi.astype(F32)).astype(BF16)
    weight = weight_ref[...]
    pre_act = jnp.dot(
        jnp.concatenate([mixed_hi, mixed_lo], axis=1), jnp.concatenate([weight, weight], axis=0),
        preferred_element_type=F32)
    sig_val = jax.nn.sigmoid(pre_act)
    acts[...] = (pre_act * sig_val).astype(BF16).reshape(acts.shape)
    cot = cot_ref[...].reshape(2 * nodes, -1).astype(F32)
    act_grad = (cot * sig_val * (1.0 + pre_act * (1.0 - sig_val))).astype(BF16)

    def weight_copy(k):
        return pltpu.make_async_remote_copy(
            src_ref=wpart.at[peer(k)], dst_ref=wincoming.at[k - 1],
            send_sem=w_send.at[k - 1], recv_sem=w_recv.at[k - 1],
            device_id={"wide": peer(k)}, device_id_type=MESH)

    weight_part = lax.dot_general(
        mixed_hi, act_grad, (((0,), (0,)), ((), ())), preferred_element_type=F32)
    for c in range(wide):
        wpart[c] = weight_part[c * share:(c + 1) * share]
    for k in order:
        weight_copy(k).start()

    back = lax.dot_general(weight, act_grad, (((1,), (1,)), ((), ())), preferred_element_type=F32).astype(BF16)

    def term_copy(k):
        return pltpu.make_async_remote_copy(
            src_ref=terms.at[k - 1], dst_ref=incoming.at[k - 1],
            send_sem=t_send.at[k - 1], recv_sem=t_recv.at[k - 1],
            device_id={"wide": peer(k)}, device_id_type=MESH)

    def send_term(k):
        terms[k - 1] = jnp.dot(back, adj[:, rows_of(peer(k))], preferred_element_type=F32).astype(BF16)
        term_copy(k).start()

    for k in order[:-1]:
        send_term(k)

    wsum = wpart[me]
    for k in order:
        weight_copy(k).wait_recv()
        wsum = wsum + wincoming[k - 1]
    nbuf[grp] = wsum

    def narrow_copy(j, slot):
        return pltpu.make_async_remote_copy(
            src_ref=nbuf.at[slot], dst_ref=nbuf.at[slot],
            send_sem=n_send.at[j - 1], recv_sem=n_recv.at[j - 1],
            device_id={"narrow": narrow_peer(j)}, device_id_type=MESH)

    for j in range(1, narrow):
        narrow_copy(j, grp).start()

    send_term(1)
    own = jnp.dot(back, adj[:, rows_of(me)], preferred_element_type=F32)
    act_ref[0] = acts[core]

    for k in order:
        term_copy(k).wait_recv()
        own = own + incoming[k - 1].astype(F32)
    fgrad_ref[0] = own.T.astype(BF16)

    for j in range(1, narrow):
        narrow_copy(j, lax.rem(grp - j + narrow, narrow)).wait_recv()
    total = nbuf[0]
    for j in range(1, narrow):
        total = total + nbuf[j]
    wgrad_ref[...] = total

    for copy in swap_copies(core, me) + [across_copy(me)]:
        copy.wait_send()
    for k in order:
        feat_copy(k, me).wait_send()
        if k > 1:
            forward_copy(k, peer(k)).wait_send()
        weight_copy(k).wait_send()
        term_copy(k).wait_send()
    for j in range(1, narrow):
        narrow_copy(j, grp).wait_send()


def hand_over(act_ref, fgrad_ref, wgrad_ref, act_out, fgrad_out, wgrad_out, sems):
    copies = [
        pltpu.make_async_copy(src, dst, sems.at[i])
        for i, (src, dst) in enumerate(((act_ref, act_out), (fgrad_ref, fgrad_out), (wgrad_ref, wgrad_out)))
    ]
    for copy in copies:
        copy.start()
    for copy in copies:
        copy.wait()


def shards(wide, narrow, features, weight, tiles, tile_cols, tile_counts, cotangent):
    _, nodes, width = features.shape
    slots, tile = tiles.shape[2:]
    zs = wide // 2
    if nodes != tile or 2 * zs != wide or zs < 4 or zs & (zs - 1):
        raise ValueError("mesh shape")
    share = width // wide
    vmem = pl.BlockSpec(memory_space=pltpu.VMEM)
    hbm = pl.BlockSpec(memory_space=pltpu.HBM)
    dma = pltpu.SemaphoreType.DMA
    flops = 2 * nodes * tile * width * (5 * wide + 8)
    results = pl.pallas_call(
        functools.partial(kernel, wide, narrow, slots),
        out_shape=(
            pltpu.VMEM((1, nodes, width), BF16),
            pltpu.VMEM((1, nodes, width), BF16),
            pltpu.VMEM((share, width), F32),
        ),
        in_specs=[hbm] * 6,
        out_specs=(vmem, vmem, vmem),
        scratch_shapes=[
            pltpu.VMEM(tile_cols.shape, jnp.int32),
            pltpu.VMEM(tile_counts.shape, jnp.int32),
            pltpu.VMEM(weight.shape, BF16),
            pltpu.VMEM((2, nodes * slots, tile), BF16),
            pltpu.VMEM((2, nodes, width), BF16),
            pltpu.VMEM((wide * tile, width), BF16),
            pltpu.VMEM((2 * nodes, wide * tile), BF16),
            pltpu.VMEM((2, nodes, width), BF16),
            pltpu.VMEM((zs - 1, width, tile), BF16),
            pltpu.VMEM((zs - 1, width, tile), BF16),
            pltpu.VMEM((wide, share, width), F32),
            pltpu.VMEM((zs - 1, share, width), F32),
            pltpu.VMEM((narrow, share, width), F32),
            dma((6,)),
            dma((zs,)), dma((zs,)),
            dma((zs - 1,)), dma((zs - 1,)),
            dma((4,)), dma((4,)),
            dma((zs - 1,)), dma((zs - 1,)),
            dma((zs - 1,)), dma((zs - 1,)),
            dma((narrow - 1,)), dma((narrow - 1,)),
        ],
        compiler_params=pltpu.CompilerParams(
            collective_id=0, has_side_effects=True, vmem_limit_bytes=VMEM_LIMIT),
        cost_estimate=pl.CostEstimate(
            flops=flops, bytes_accessed=2 * nodes * width * (slots + 4), transcendentals=2 * nodes * width),
        name="graph_layer",
    )(*(pltpu.with_memory_space_constraint(x, pltpu.HBM) for x in (
        tile_cols, tile_counts, features, weight, tiles.reshape(nodes * slots, tile), cotangent)))
    return pl.pallas_call(
        hand_over,
        out_shape=tuple(jax.ShapeDtypeStruct(r.shape, r.dtype) for r in results),
        in_specs=[vmem] * 3,
        out_specs=(hbm,) * 3,
        scratch_shapes=[dma((3,))],
        compiler_params=pltpu.CompilerParams(vmem_limit_bytes=2 * 1024 * 1024),
        name="hand_over",
    )(*(pltpu.with_memory_space_constraint(r, pltpu.VMEM) for r in results))


def solution(mesh):
    placed = (
        P("narrow", "wide", None),
        P(),
        P("narrow", "wide", None, None),
        P("narrow", None, None),
        P("narrow", None),
        P("narrow", "wide", None),
    )
    return jax.shard_map(
        functools.partial(shards, mesh.shape["wide"], mesh.shape["narrow"]),
        mesh=mesh,
        in_specs=placed,
        out_specs=(P("narrow", "wide", None), P("narrow", "wide", None), P("wide", None)),
        check_vma=False,
    )
```

```python
import functools

import jax
import jax.numpy as jnp
from jax import lax
from jax.experimental import pallas as pl
from jax.experimental.pallas import tpu as pltpu
from jax.sharding import PartitionSpec as P

MESH = pl.DeviceIdType.MESH
F32 = jnp.float32
BF16 = jnp.bfloat16
VMEM_LIMIT = 32 * 1024 * 1024


def selection(cols_ref, counts_ref, row_block, blocks, slots, chunk):
    shape = (blocks * chunk, chunk * slots)
    row = lax.broadcasted_iota(jnp.int32, shape, 0)
    lane = lax.broadcasted_iota(jnp.int32, (1, chunk * slots), 1)
    slot = lax.rem(lane, slots)
    node = lane // slots
    counts = counts_ref[...]
    here = lax.broadcasted_iota(jnp.int32, counts.shape, 1) == row_block
    count = jnp.sum(jnp.where(here, counts, 0), axis=1, keepdims=True)
    cols = cols_ref[0, pl.ds(row_block, 1), :]
    wanted = jnp.zeros((1, chunk * slots), jnp.int32)
    for s in range(slots):
        wanted = jnp.where(slot == s, cols[:, s:s + 1], wanted)
    wanted = jnp.where(slot < count, wanted * chunk + node, -1)
    return jnp.where(row == wanted, 1.0, 0.0).astype(BF16)


def partner(z, k):
    bit, out = 1, z
    while bit <= k:
        if k & bit:
            out = out + bit - 2 * bit * lax.rem(z // bit, 2)
        bit *= 2
    return out


def partner_order(count):
    order, half = [], count // 2
    while half:
        order += list(range(half, 2 * half))
        half //= 2
    return order


def kernel(
    wide, narrow, slots,
    cols_hbm, counts_hbm, feat_hbm, weight_hbm, tiles_hbm, cot_hbm,
    act_ref, fgrad_ref, wgrad_ref,
    cols_ref, counts_ref, weight_ref, tiles_ref, cot_ref, gathered, adj, acts, terms, incoming, wpart, wincoming, nbuf,
    in_sems, f_send, f_recv, x_send, x_recv, s_send, s_recv, t_send, t_recv, w_send, w_recv, n_send, n_recv,
):
    me = lax.axis_index("wide")
    grp = lax.axis_index("narrow")
    zs = wide // 2
    z, core = me // 2, lax.rem(me, 2)
    other = 1 - core
    sibling = 2 * z + other
    across = 2 * partner(z, 1) + other
    nodes = feat_hbm.shape[1]
    tile = tiles_hbm.shape[1]
    chunk = tile // slots
    share = wgrad_ref.shape[0]
    order = partner_order(zs)

    def peer(k):
        return 2 * partner(z, k) + core

    def narrow_peer(j):
        return lax.rem(grp + j, narrow)

    barrier = pltpu.get_barrier_semaphore()
    for k in order:
        pl.semaphore_signal(barrier, inc=1, device_id={"wide": peer(k)}, device_id_type=MESH)
    for device in (sibling, across):
        pl.semaphore_signal(barrier, inc=1, device_id={"wide": device}, device_id_type=MESH)
    for j in range(1, narrow):
        pl.semaphore_signal(barrier, inc=1, device_id={"narrow": narrow_peer(j)}, device_id_type=MESH)

    def rows_of(index):
        return pl.ds(pl.multiple_of(index * tile, tile), tile)

    loads = [
        pltpu.make_async_copy(src, dst, in_sems.at[i])
        for i, (src, dst) in enumerate((
            (feat_hbm.at[0], gathered.at[rows_of(me)]),
            (cols_hbm, cols_ref), (counts_hbm, counts_ref), (tiles_hbm, tiles_ref.at[core]), (weight_hbm, weight_ref),
            (cot_hbm.at[0], cot_ref.at[core])))
    ]
    for load in loads:
        load.start()
    loads[0].wait()
    pl.semaphore_wait(barrier, zs + narrow)

    def feat_copy(k, slot):
        return pltpu.make_async_remote_copy(
            src_ref=gathered.at[rows_of(me)], dst_ref=gathered.at[rows_of(slot)],
            send_sem=f_send.at[k - 1], recv_sem=f_recv.at[k - 1],
            device_id={"wide": peer(k)}, device_id_type=MESH)

    def across_copy(slot):
        return pltpu.make_async_remote_copy(
            src_ref=gathered.at[rows_of(me)], dst_ref=gathered.at[rows_of(slot)],
            send_sem=f_send.at[zs - 1], recv_sem=f_recv.at[zs - 1],
            device_id={"wide": across}, device_id_type=MESH)

    def forward_copy(k, slot):
        return pltpu.make_async_remote_copy(
            src_ref=gathered.at[rows_of(slot)], dst_ref=gathered.at[rows_of(slot)],
            send_sem=x_send.at[k - 1], recv_sem=x_recv.at[k - 1],
            device_id={"wide": sibling}, device_id_type=MESH)

    def swap_copies(half, slot):
        piece = nodes * slots // 2
        pairs = [(tiles_hbm.at[pl.ds(i * piece, piece)], tiles_ref.at[half, pl.ds(i * piece, piece)]) for i in range(2)]
        pairs += [(gathered.at[rows_of(slot)], gathered.at[rows_of(slot)]), (cot_hbm.at[0], cot_ref.at[half])]
        return [
            pltpu.make_async_remote_copy(
                src_ref=src, dst_ref=dst, send_sem=s_send.at[i], recv_sem=s_recv.at[i],
                device_id={"wide": sibling}, device_id_type=MESH)
            for i, (src, dst) in enumerate(pairs)
        ]

    outgoing = swap_copies(core, me)
    for k in order[:-1]:
        feat_copy(k, me).start()
    outgoing[0].start()
    outgoing[1].start()
    feat_copy(1, me).start()
    across_copy(me).start()
    outgoing[2].start()
    outgoing[3].start()
    for load in loads[1:4]:
        load.wait()

    def build(half, pick, piece):
        count = nodes // chunk // 2
        for j in range(piece * count, (piece + 1) * count, 2):
            both = jnp.concatenate(
                [tiles_ref[half, i * tile:(i + 1) * tile, :] for i in (j, j + 1)], axis=1)
            part = jnp.dot(pick, both, preferred_element_type=F32).astype(BF16)
            for i in range(2):
                rows = pl.ds(pl.multiple_of(half * nodes + (j + i) * chunk, chunk), chunk)
                for c in range(wide):
                    adj[rows, c * tile:(c + 1) * tile] = part[
                        c * chunk:(c + 1) * chunk, i * tile:(i + 1) * tile]

    def mix(chip):
        span = pl.ds(pl.multiple_of(chip * 2 * tile, 2 * tile), 2 * tile)
        return jnp.dot(adj[:, span], gathered[span, :], preferred_element_type=F32)

    pick = selection(cols_ref, counts_ref, 2 * z + core, wide, slots, chunk)
    build(core, pick, 0)
    build(core, pick, 1)
    pick = selection(cols_ref, counts_ref, 2 * z + other, wide, slots, chunk)
    swapped = swap_copies(other, sibling)
    feat_copy(order[0], peer(order[0])).wait_recv()
    forward_copy(order[0], peer(order[0])).start()
    for piece in range(2):
        swapped[piece].wait_recv()
        build(other, pick, piece)
    for k in order[1:-1]:
        feat_copy(k, peer(k)).wait_recv()
        forward_copy(k, peer(k)).start()
    for load in loads[4:]:
        load.wait()
    swapped[2].wait_recv()
    swapped[3].wait_recv()
    mixed = mix(z)
    feat_copy(1, peer(1)).wait_recv()
    across_copy(across).wait_recv()
    mixed = mixed + mix(partner(z, 1))
    for k in order[:-1]:
        forward_copy(k, 2 * partner(z, k) + other).wait_recv()
        mixed = mixed + mix(partner(z, k))
    mixed_hi = mixed.astype(BF16)
    mixed_lo = (mixed - mixed_hi.astype(F32)).astype(BF16)
    weight = weight_ref[...]
    pre_act = jnp.dot(
        jnp.concatenate([mixed_hi, mixed_lo], axis=1), jnp.concatenate([weight, weight], axis=0),
        preferred_element_type=F32)
    sig_val = jax.nn.sigmoid(pre_act)
    acts[...] = (pre_act * sig_val).astype(BF16).reshape(acts.shape)
    cot = cot_ref[...].reshape(2 * nodes, -1).astype(F32)
    act_grad = (cot * sig_val * (1.0 + pre_act * (1.0 - sig_val))).astype(BF16)

    def weight_copy(k):
        return pltpu.make_async_remote_copy(
            src_ref=wpart.at[peer(k)], dst_ref=wincoming.at[k - 1],
            send_sem=w_send.at[k - 1], recv_sem=w_recv.at[k - 1],
            device_id={"wide": peer(k)}, device_id_type=MESH)

    back = lax.dot_general(weight, act_grad, (((1,), (1,)), ((), ())), preferred_element_type=F32).astype(BF16)

    def term_copy(k):
        return pltpu.make_async_remote_copy(
            src_ref=terms.at[k - 1], dst_ref=incoming.at[k - 1],
            send_sem=t_send.at[k - 1], recv_sem=t_recv.at[k - 1],
            device_id={"wide": peer(k)}, device_id_type=MESH)

    def send_term(k):
        terms[k - 1] = jnp.dot(back, adj[:, rows_of(peer(k))], preferred_element_type=F32).astype(BF16)
        term_copy(k).start()

    send_term(order[0])
    weight_part = lax.dot_general(
        mixed_hi, act_grad, (((0,), (0,)), ((), ())), preferred_element_type=F32)
    for c in range(wide):
        wpart[c] = weight_part[c * share:(c + 1) * share]
    for k in order:
        weight_copy(k).start()

    for k in order[1:-1]:
        send_term(k)

    wsum = wpart[me]
    for k in order:
        weight_copy(k).wait_recv()
        wsum = wsum + wincoming[k - 1]
    nbuf[grp] = wsum

    def narrow_copy(j, slot):
        return pltpu.make_async_remote_copy(
            src_ref=nbuf.at[slot], dst_ref=nbuf.at[slot],
            send_sem=n_send.at[j - 1], recv_sem=n_recv.at[j - 1],
            device_id={"narrow": narrow_peer(j)}, device_id_type=MESH)

    for j in range(1, narrow):
        narrow_copy(j, grp).start()

    send_term(1)
    own = jnp.dot(back, adj[:, rows_of(me)], preferred_element_type=F32)
    act_ref[0] = acts[core]

    for k in order:
        term_copy(k).wait_recv()
        own = own + incoming[k - 1].astype(F32)
    fgrad_ref[0] = own.T.astype(BF16)

    for j in range(1, narrow):
        narrow_copy(j, lax.rem(grp - j + narrow, narrow)).wait_recv()
    total = nbuf[0]
    for j in range(1, narrow):
        total = total + nbuf[j]
    wgrad_ref[...] = total

    for copy in swap_copies(core, me) + [across_copy(me)]:
        copy.wait_send()
    for k in order:
        feat_copy(k, me).wait_send()
        if k > 1:
            forward_copy(k, peer(k)).wait_send()
        weight_copy(k).wait_send()
        term_copy(k).wait_send()
    for j in range(1, narrow):
        narrow_copy(j, grp).wait_send()


def hand_over(act_ref, fgrad_ref, wgrad_ref, act_out, fgrad_out, wgrad_out, sems):
    copies = [
        pltpu.make_async_copy(src, dst, sems.at[i])
        for i, (src, dst) in enumerate(((act_ref, act_out), (fgrad_ref, fgrad_out), (wgrad_ref, wgrad_out)))
    ]
    for copy in copies:
        copy.start()
    for copy in copies:
        copy.wait()


def shards(wide, narrow, features, weight, tiles, tile_cols, tile_counts, cotangent):
    _, nodes, width = features.shape
    slots, tile = tiles.shape[2:]
    zs = wide // 2
    if nodes != tile or 2 * zs != wide or zs < 4 or zs & (zs - 1):
        raise ValueError("mesh shape")
    share = width // wide
    vmem = pl.BlockSpec(memory_space=pltpu.VMEM)
    hbm = pl.BlockSpec(memory_space=pltpu.HBM)
    dma = pltpu.SemaphoreType.DMA
    flops = 2 * nodes * tile * width * (5 * wide + 8)
    results = pl.pallas_call(
        functools.partial(kernel, wide, narrow, slots),
        out_shape=(
            pltpu.VMEM((1, nodes, width), BF16),
            pltpu.VMEM((1, nodes, width), BF16),
            pltpu.VMEM((share, width), F32),
        ),
        in_specs=[hbm] * 6,
        out_specs=(vmem, vmem, vmem),
        scratch_shapes=[
            pltpu.VMEM(tile_cols.shape, jnp.int32),
            pltpu.VMEM(tile_counts.shape, jnp.int32),
            pltpu.VMEM(weight.shape, BF16),
            pltpu.VMEM((2, nodes * slots, tile), BF16),
            pltpu.VMEM((2, nodes, width), BF16),
            pltpu.VMEM((wide * tile, width), BF16),
            pltpu.VMEM((2 * nodes, wide * tile), BF16),
            pltpu.VMEM((2, nodes, width), BF16),
            pltpu.VMEM((zs - 1, width, tile), BF16),
            pltpu.VMEM((zs - 1, width, tile), BF16),
            pltpu.VMEM((wide, share, width), F32),
            pltpu.VMEM((zs - 1, share, width), F32),
            pltpu.VMEM((narrow, share, width), F32),
            dma((6,)),
            dma((zs,)), dma((zs,)),
            dma((zs - 1,)), dma((zs - 1,)),
            dma((4,)), dma((4,)),
            dma((zs - 1,)), dma((zs - 1,)),
            dma((zs - 1,)), dma((zs - 1,)),
            dma((narrow - 1,)), dma((narrow - 1,)),
        ],
        compiler_params=pltpu.CompilerParams(
            collective_id=0, has_side_effects=True, vmem_limit_bytes=VMEM_LIMIT),
        cost_estimate=pl.CostEstimate(
            flops=flops, bytes_accessed=2 * nodes * width * (slots + 4), transcendentals=2 * nodes * width),
        name="graph_layer",
    )(*(pltpu.with_memory_space_constraint(x, pltpu.HBM) for x in (
        tile_cols, tile_counts, features, weight, tiles.reshape(nodes * slots, tile), cotangent)))
    return pl.pallas_call(
        hand_over,
        out_shape=tuple(jax.ShapeDtypeStruct(r.shape, r.dtype) for r in results),
        in_specs=[vmem] * 3,
        out_specs=(hbm,) * 3,
        scratch_shapes=[dma((3,))],
        compiler_params=pltpu.CompilerParams(vmem_limit_bytes=2 * 1024 * 1024),
        name="hand_over",
    )(*(pltpu.with_memory_space_constraint(r, pltpu.VMEM) for r in results))


def solution(mesh):
    placed = (
        P("narrow", "wide", None),
        P(),
        P("narrow", "wide", None, None),
        P("narrow", None, None),
        P("narrow", None),
        P("narrow", "wide", None),
    )
    return jax.shard_map(
        functools.partial(shards, mesh.shape["wide"], mesh.shape["narrow"]),
        mesh=mesh,
        in_specs=placed,
        out_specs=(P("narrow", "wide", None), P("narrow", "wide", None), P("wide", None)),
        check_vma=False,
    )
```

```python
import functools

import jax
import jax.numpy as jnp
from jax import lax
from jax.experimental import pallas as pl
from jax.experimental.pallas import tpu as pltpu
from jax.sharding import PartitionSpec as P

MESH = pl.DeviceIdType.MESH
F32 = jnp.float32
BF16 = jnp.bfloat16
VMEM_LIMIT = 32 * 1024 * 1024


def selection(cols_ref, counts_ref, row_block, blocks, slots, chunk):
    shape = (blocks * chunk, chunk * slots)
    row = lax.broadcasted_iota(jnp.int32, shape, 0)
    lane = lax.broadcasted_iota(jnp.int32, (1, chunk * slots), 1)
    slot = lax.rem(lane, slots)
    node = lane // slots
    counts = counts_ref[...]
    here = lax.broadcasted_iota(jnp.int32, counts.shape, 1) == row_block
    count = jnp.sum(jnp.where(here, counts, 0), axis=1, keepdims=True)
    cols = cols_ref[0, pl.ds(row_block, 1), :]
    wanted = jnp.zeros((1, chunk * slots), jnp.int32)
    for s in range(slots):
        wanted = jnp.where(slot == s, cols[:, s:s + 1], wanted)
    wanted = jnp.where(slot < count, wanted * chunk + node, -1)
    return jnp.where(row == wanted, 1.0, 0.0).astype(BF16)


def partner(z, k):
    bit, out = 1, z
    while bit <= k:
        if k & bit:
            out = out + bit - 2 * bit * lax.rem(z // bit, 2)
        bit *= 2
    return out


def partner_order(count):
    order, half = [], count // 2
    while half:
        order += list(range(half, 2 * half))
        half //= 2
    return order


def kernel(
    wide, narrow, slots,
    cols_hbm, counts_hbm, feat_hbm, weight_hbm, tiles_hbm, cot_hbm,
    act_ref, fgrad_ref, wgrad_ref,
    cols_ref, counts_ref, weight_ref, tiles_ref, cot_ref, gathered, adj, acts, terms, incoming, wpart, wincoming, nbuf,
    in_sems, f_send, f_recv, x_send, x_recv, s_send, s_recv, t_send, t_recv, w_send, w_recv, n_send, n_recv,
):
    me = lax.axis_index("wide")
    grp = lax.axis_index("narrow")
    zs = wide // 2
    z, core = me // 2, lax.rem(me, 2)
    other = 1 - core
    sibling = 2 * z + other
    across = 2 * partner(z, 1) + other
    nodes = feat_hbm.shape[1]
    tile = tiles_hbm.shape[1]
    chunk = tile // slots
    share = wgrad_ref.shape[0]
    order = partner_order(zs)

    def peer(k):
        return 2 * partner(z, k) + core

    def narrow_peer(j):
        return lax.rem(grp + j, narrow)

    barrier = pltpu.get_barrier_semaphore()
    for k in order:
        pl.semaphore_signal(barrier, inc=1, device_id={"wide": peer(k)}, device_id_type=MESH)
    for device in (sibling, across):
        pl.semaphore_signal(barrier, inc=1, device_id={"wide": device}, device_id_type=MESH)
    for j in range(1, narrow):
        pl.semaphore_signal(barrier, inc=1, device_id={"narrow": narrow_peer(j)}, device_id_type=MESH)

    def rows_of(index):
        return pl.ds(pl.multiple_of(index * tile, tile), tile)

    loads = [
        pltpu.make_async_copy(src, dst, in_sems.at[i])
        for i, (src, dst) in enumerate((
            (feat_hbm.at[0], gathered.at[rows_of(me)]),
            (cols_hbm, cols_ref), (counts_hbm, counts_ref), (tiles_hbm, tiles_ref.at[core]), (weight_hbm, weight_ref),
            (cot_hbm.at[0], cot_ref.at[core])))
    ]
    for load in loads:
        load.start()
    loads[0].wait()
    pl.semaphore_wait(barrier, zs + narrow)

    def feat_copy(k, slot):
        return pltpu.make_async_remote_copy(
            src_ref=gathered.at[rows_of(me)], dst_ref=gathered.at[rows_of(slot)],
            send_sem=f_send.at[k - 1], recv_sem=f_recv.at[k - 1],
            device_id={"wide": peer(k)}, device_id_type=MESH)

    def across_copy(slot):
        return pltpu.make_async_remote_copy(
            src_ref=gathered.at[rows_of(me)], dst_ref=gathered.at[rows_of(slot)],
            send_sem=f_send.at[zs - 1], recv_sem=f_recv.at[zs - 1],
            device_id={"wide": across}, device_id_type=MESH)

    def forward_copy(k, slot):
        return pltpu.make_async_remote_copy(
            src_ref=gathered.at[rows_of(slot)], dst_ref=gathered.at[rows_of(slot)],
            send_sem=x_send.at[k - 1], recv_sem=x_recv.at[k - 1],
            device_id={"wide": sibling}, device_id_type=MESH)

    def swap_copies(half, slot):
        piece = nodes * slots // 2
        pairs = [(tiles_hbm.at[pl.ds(i * piece, piece)], tiles_ref.at[half, pl.ds(i * piece, piece)]) for i in range(2)]
        pairs += [(gathered.at[rows_of(slot)], gathered.at[rows_of(slot)]), (cot_hbm.at[0], cot_ref.at[half])]
        return [
            pltpu.make_async_remote_copy(
                src_ref=src, dst_ref=dst, send_sem=s_send.at[i], recv_sem=s_recv.at[i],
                device_id={"wide": sibling}, device_id_type=MESH)
            for i, (src, dst) in enumerate(pairs)
        ]

    outgoing = swap_copies(core, me)
    for k in order[:-1]:
        feat_copy(k, me).start()
    outgoing[0].start()
    outgoing[1].start()
    feat_copy(1, me).start()
    across_copy(me).start()
    outgoing[2].start()
    outgoing[3].start()
    for load in loads[1:4]:
        load.wait()

    def build(half, pick, piece):
        count = nodes // chunk // 2
        for j in range(piece * count, (piece + 1) * count, 2):
            both = jnp.concatenate(
                [tiles_ref[half, i * tile:(i + 1) * tile, :] for i in (j, j + 1)], axis=1)
            part = jnp.dot(pick, both, preferred_element_type=F32).astype(BF16)
            for i in range(2):
                rows = pl.ds(pl.multiple_of(half * nodes + (j + i) * chunk, chunk), chunk)
                for c in range(wide):
                    adj[rows, c * tile:(c + 1) * tile] = part[
                        c * chunk:(c + 1) * chunk, i * tile:(i + 1) * tile]

    def mix(chip):
        span = pl.ds(pl.multiple_of(chip * 2 * tile, 2 * tile), 2 * tile)
        return jnp.dot(adj[:, span], gathered[span, :], preferred_element_type=F32)

    pick = selection(cols_ref, counts_ref, 2 * z + core, wide, slots, chunk)
    build(core, pick, 0)
    build(core, pick, 1)
    pick = selection(cols_ref, counts_ref, 2 * z + other, wide, slots, chunk)
    swapped = swap_copies(other, sibling)
    feat_copy(order[0], peer(order[0])).wait_recv()
    forward_copy(order[0], peer(order[0])).start()
    for piece in range(2):
        swapped[piece].wait_recv()
        build(other, pick, piece)
    for k in order[1:-1]:
        feat_copy(k, peer(k)).wait_recv()
        forward_copy(k, peer(k)).start()
    for load in loads[4:]:
        load.wait()
    swapped[2].wait_recv()
    swapped[3].wait_recv()
    mixed = mix(z)
    feat_copy(1, peer(1)).wait_recv()
    across_copy(across).wait_recv()
    mixed = mixed + mix(partner(z, 1))
    for k in order[:-1]:
        forward_copy(k, 2 * partner(z, k) + other).wait_recv()
        mixed = mixed + mix(partner(z, k))
    mixed_hi = mixed.astype(BF16)
    mixed_lo = (mixed - mixed_hi.astype(F32)).astype(BF16)
    weight = weight_ref[...]
    pre_act = jnp.dot(
        jnp.concatenate([mixed_hi, mixed_lo], axis=1), jnp.concatenate([weight, weight], axis=0),
        preferred_element_type=F32)
    sig_val = jax.nn.sigmoid(pre_act)
    acts[...] = (pre_act * sig_val).astype(BF16).reshape(acts.shape)
    cot = cot_ref[...].reshape(2 * nodes, -1).astype(F32)
    act_grad = (cot * sig_val * (1.0 + pre_act * (1.0 - sig_val))).astype(BF16)

    def weight_copy(k):
        return pltpu.make_async_remote_copy(
            src_ref=wpart.at[peer(k)], dst_ref=wincoming.at[k - 1],
            send_sem=w_send.at[k - 1], recv_sem=w_recv.at[k - 1],
            device_id={"wide": peer(k)}, device_id_type=MESH)

    weight_part = lax.dot_general(
        mixed_hi, act_grad, (((0,), (0,)), ((), ())), preferred_element_type=F32)
    for c in range(wide):
        wpart[c] = weight_part[c * share:(c + 1) * share]
    for k in order:
        weight_copy(k).start()

    back = lax.dot_general(weight, act_grad, (((1,), (1,)), ((), ())), preferred_element_type=F32).astype(BF16)

    def term_copy(k):
        return pltpu.make_async_remote_copy(
            src_ref=terms.at[k - 1], dst_ref=incoming.at[k - 1],
            send_sem=t_send.at[k - 1], recv_sem=t_recv.at[k - 1],
            device_id={"wide": peer(k)}, device_id_type=MESH)

    def send_term(k):
        terms[k - 1] = jnp.dot(back, adj[:, rows_of(peer(k))], preferred_element_type=F32).astype(BF16)
        term_copy(k).start()

    for k in order[:-1]:
        send_term(k)

    wsum = wpart[me]
    for k in order:
        weight_copy(k).wait_recv()
        wsum = wsum + wincoming[k - 1]
    nbuf[grp] = wsum

    def narrow_copy(j, slot):
        return pltpu.make_async_remote_copy(
            src_ref=nbuf.at[slot], dst_ref=nbuf.at[slot],
            send_sem=n_send.at[j - 1], recv_sem=n_recv.at[j - 1],
            device_id={"narrow": narrow_peer(j)}, device_id_type=MESH)

    for j in range(1, narrow):
        narrow_copy(j, grp).start()

    send_term(1)
    own = jnp.dot(back, adj[:, rows_of(me)], preferred_element_type=F32)
    act_ref[0] = acts[core]

    for k in order:
        term_copy(k).wait_recv()
        own = own + incoming[k - 1].astype(F32)
    fgrad_ref[0] = own.T.astype(BF16)

    for j in range(1, narrow):
        narrow_copy(j, lax.rem(grp - j + narrow, narrow)).wait_recv()
    total = nbuf[0]
    for j in range(1, narrow):
        total = total + nbuf[j]
    wgrad_ref[...] = total

    for copy in swap_copies(core, me) + [across_copy(me)]:
        copy.wait_send()
    for k in order:
        feat_copy(k, me).wait_send()
        if k > 1:
            forward_copy(k, peer(k)).wait_send()
        weight_copy(k).wait_send()
        term_copy(k).wait_send()
    for j in range(1, narrow):
        narrow_copy(j, grp).wait_send()


def hand_over(act_ref, fgrad_ref, wgrad_ref, act_out, fgrad_out, wgrad_out, sems):
    copies = [
        pltpu.make_async_copy(src, dst, sems.at[i])
        for i, (src, dst) in enumerate(((act_ref, act_out), (fgrad_ref, fgrad_out), (wgrad_ref, wgrad_out)))
    ]
    for copy in copies:
        copy.start()
    for copy in copies:
        copy.wait()


def shards(wide, narrow, features, weight, tiles, tile_cols, tile_counts, cotangent):
    _, nodes, width = features.shape
    slots, tile = tiles.shape[2:]
    zs = wide // 2
    if nodes != tile or 2 * zs != wide or zs < 4 or zs & (zs - 1):
        raise ValueError("mesh shape")
    share = width // wide
    vmem = pl.BlockSpec(memory_space=pltpu.VMEM)
    hbm = pl.BlockSpec(memory_space=pltpu.HBM)
    dma = pltpu.SemaphoreType.DMA
    flops = 2 * nodes * tile * width * (5 * wide + 8)
    results = pl.pallas_call(
        functools.partial(kernel, wide, narrow, slots),
        out_shape=(
            pltpu.VMEM((1, nodes, width), BF16),
            pltpu.VMEM((1, nodes, width), BF16),
            pltpu.VMEM((share, width), F32),
        ),
        in_specs=[hbm] * 6,
        out_specs=(vmem, vmem, vmem),
        scratch_shapes=[
            pltpu.VMEM(tile_cols.shape, jnp.int32),
            pltpu.VMEM(tile_counts.shape, jnp.int32),
            pltpu.VMEM(weight.shape, BF16),
            pltpu.VMEM((2, nodes * slots, tile), BF16),
            pltpu.VMEM((2, nodes, width), BF16),
            pltpu.VMEM((wide * tile, width), BF16),
            pltpu.VMEM((2 * nodes, wide * tile), BF16),
            pltpu.VMEM((2, nodes, width), BF16),
            pltpu.VMEM((zs - 1, width, tile), BF16),
            pltpu.VMEM((zs - 1, width, tile), BF16),
            pltpu.VMEM((wide, share, width), F32),
            pltpu.VMEM((zs - 1, share, width), F32),
            pltpu.VMEM((narrow, share, width), F32),
            dma((6,)),
            dma((zs,)), dma((zs,)),
            dma((zs - 1,)), dma((zs - 1,)),
            dma((4,)), dma((4,)),
            dma((zs - 1,)), dma((zs - 1,)),
            dma((zs - 1,)), dma((zs - 1,)),
            dma((narrow - 1,)), dma((narrow - 1,)),
        ],
        compiler_params=pltpu.CompilerParams(
            collective_id=0, has_side_effects=True, vmem_limit_bytes=VMEM_LIMIT),
        cost_estimate=pl.CostEstimate(
            flops=flops, bytes_accessed=2 * nodes * width * (slots + 4), transcendentals=2 * nodes * width),
        name="graph_layer",
    )(*(pltpu.with_memory_space_constraint(x, pltpu.HBM) for x in (
        tile_cols, tile_counts, features, weight, tiles.reshape(nodes * slots, tile), cotangent)))
    return pl.pallas_call(
        hand_over,
        out_shape=tuple(jax.ShapeDtypeStruct(r.shape, r.dtype) for r in results),
        in_specs=[vmem] * 3,
        out_specs=(hbm,) * 3,
        scratch_shapes=[dma((3,))],
        compiler_params=pltpu.CompilerParams(vmem_limit_bytes=2 * 1024 * 1024),
        name="hand_over",
    )(*(pltpu.with_memory_space_constraint(r, pltpu.VMEM) for r in results))


def solution(mesh):
    placed = (
        P("narrow", "wide", None),
        P(),
        P("narrow", "wide", None, None),
        P("narrow", None, None),
        P("narrow", None),
        P("narrow", "wide", None),
    )
    return jax.shard_map(
        functools.partial(shards, mesh.shape["wide"], mesh.shape["narrow"]),
        mesh=mesh,
        in_specs=placed,
        out_specs=(P("narrow", "wide", None), P("narrow", "wide", None), P("wide", None)),
        check_vma=False,
    )
```
